256 devices in a mesh: gy: 16 (over y, x), gz: 16 (over z, core).
Axes of the slice: x: 4, y: 4, z: 8, core: 2. Of those that a mesh axis runs over, the one named last changes fastest.
Arguments:
- right_side: float32 [256, 256, 512], P('gz', 'gy'), may hold values from -6 to 6
- cotangent: float32 [256, 256, 512], P('gz', 'gy'), may hold values from -6 to 6
- phase: int32 [256, 256, 512], P('gz', 'gy'), may hold values 0 or 1
Outputs:
- correction: float32 [256, 256, 512], P('gz', 'gy')
- transposed: float32 [256, 256, 512], P('gz', 'gy')
The draws below stay inside these ranges and needn't reach their ends.
All inputs are finite; a program needn't handle non-finite values. No bound on the sum of `phase` on one device may be relied on, other than what follows from the above.
Results may differ from the reference program's by a relative error of at most 0.0001.
Values sent between devices are 32-bit elements; how exact they have to be, the bound alone decides.
A program may use at most 192 MiB of HBM per device.

```python
import jax
import jax.numpy as jnp

NX = 512
LEVELS = 7
BEFORE_SWEEPS = 2
AFTER_SWEEPS = 1
COARSE_SWEEPS = 4
NZ = 256
NY = 256


def draw_right_side(key, part):
    key = jax.random.fold_in(key, 11)
    return jnp.clip(jax.random.normal(key, (NZ, NY, NX), jnp.float32), -6.0, 6.0)


def draw_cotangent(key, part):
    key = jax.random.fold_in(key, 12)
    return jnp.clip(jax.random.normal(key, (NZ, NY, NX), jnp.float32), -6.0, 6.0)


def place_ends(array, key, smallest, high):
    index_at = [jax.random.randint(jax.random.fold_in(key, axis), (), 0, length) for axis, length in enumerate(array.shape)]
    longest = array.shape.index(max(array.shape))
    beside = index_at[:longest] + [(index_at[longest] + 1) % array.shape[longest]] + index_at[longest + 1:]
    return array.at[tuple(index_at)].set(smallest).at[tuple(beside)].set(high)


def setup_inputs(seed: int = 0) -> dict:
    key_of = jax.random.split(jax.random.key(seed), 4)
    right_side = draw_right_side(jax.random.fold_in(key_of[3], 71), 0)
    cotangent = draw_cotangent(jax.random.fold_in(key_of[3], 71), 0)
    phase = place_ends((jax.random.randint(key_of[2], (NZ, NY, NX), 0, 5) < 2).astype(jnp.int32), jax.random.fold_in(key_of[2], 1), 0, 1)
    return {"right_side": right_side, "cotangent": cotangent, "phase": phase}


light_density = 1.0
heavy_density = 8.0
spectrum_mid = 1.125
spectrum_half = 0.875
spectrum_ratio = 1.125 / 0.875


def neighbours(values):
    padded_z = jnp.pad(values, ((1, 1), (0, 0), (0, 0)))
    return (padded_z[:-2], padded_z[2:], jnp.roll(values, 1, 1), jnp.roll(values, -1, 1), jnp.roll(values, 1, 2), jnp.roll(values, -1, 2))


def operator_terms(mobility, scale):
    face_terms = tuple(0.5 * scale * (mobility + other) for other in neighbours(mobility))
    diagonal = face_terms[0]
    for other in face_terms[1:]:
        diagonal = diagonal + other
    return face_terms, diagonal


def apply_operator(values, terms):
    face_terms, diagonal = terms
    result = diagonal * values
    for weight, other in zip(face_terms, neighbours(values)):
        result = result - weight * other
    return result


def chebyshev(source, terms, count_of):
    inverse = 1.0 / terms[1]
    direction = inverse * source / spectrum_mid
    iterate = direction
    factor = 1.0 / spectrum_ratio
    for sweep_at in range(1, count_of):
        remainder = source - apply_operator(iterate, terms)
        new_factor = 1.0 / (2.0 * spectrum_ratio - factor)
        direction = (new_factor * factor) * direction + (2.0 * new_factor / spectrum_half) * inverse * remainder
        iterate = iterate + direction
        factor = new_factor
    return iterate


def restrict(values):
    depth_z, depth_y, depth_x = values.shape
    return values.reshape(depth_z // 2, 2, depth_y // 2, 2, depth_x // 2, 2).mean(axis=(1, 3, 5))


def prolong(values):
    return jnp.repeat(jnp.repeat(jnp.repeat(values, 2, 0), 2, 1), 2, 2)


def vcycle(source, depth_at, ladder, before_count, after_count):
    terms = ladder[depth_at]
    if depth_at == len(ladder) - 1:
        return chebyshev(source, terms, COARSE_SWEEPS)
    smoothed = chebyshev(source, terms, before_count)
    remainder = source - apply_operator(smoothed, terms)
    coarse_fix = vcycle(restrict(remainder), depth_at + 1, ladder, before_count, after_count)
    corrected = smoothed + prolong(coarse_fix)
    return corrected + chebyshev(source - apply_operator(corrected, terms), terms, after_count)


def reference(right_side, cotangent, phase):
    mobility = jnp.where(phase == 1, 1.0 / heavy_density, 1.0 / light_density).astype(jnp.float32)
    ladder = []
    for depth_at in range(LEVELS):
        ladder.append(operator_terms(mobility, 0.25 ** depth_at))
        if depth_at + 1 < LEVELS:
            mobility = restrict(mobility)
    correction = vcycle(right_side, 0, ladder, BEFORE_SWEEPS, AFTER_SWEEPS)
    transposed = vcycle(cotangent, 0, ladder, AFTER_SWEEPS, BEFORE_SWEEPS)
    return correction, transposed
```

```python
import functools

import jax
import jax.numpy as jnp
from jax import lax
from jax.experimental import pallas as pl
from jax.experimental.pallas import tpu as pltpu
from jax.sharding import PartitionSpec as P

MESH = pl.DeviceIdType.MESH
RING = 16
MID = 1.125
HALF = 0.875
RATIO = MID / HALF
FIRST = 1.0 / RATIO
SECOND = 1.0 / (2.0 * RATIO - FIRST)
C1 = SECOND * FIRST
C2 = 2.0 * SECOND / HALF
LIGHT = 1.0
HEAVY = 1.0 / 8.0
AROUND = tuple((a, b) for a in (-1, 0, 1) for b in (-1, 0, 1) if (a, b) != (0, 0))
F32 = jnp.float32


def flat(values):
    return values.reshape((-1,) + values.shape[-2:])


def sub_iota(shape):
    return lax.broadcasted_iota(jnp.int32, shape, len(shape) - 2)


def lane_iota(shape):
    return lax.broadcasted_iota(jnp.int32, shape, len(shape) - 1)


def sub_take(values, index_of):
    rows = flat(values)
    if rows.shape[0] == 1:
        rows = rows[0]
    index = index_of(sub_iota(rows.shape))
    return jnp.take_along_axis(rows, index, axis=rows.ndim - 2).reshape(values.shape)


def lane_take(values, index_of):
    rows = flat(values)
    if rows.shape[0] == 1:
        rows = rows[0]
    index = index_of(sub_iota(rows.shape), lane_iota(rows.shape))
    return jnp.take_along_axis(rows, index, axis=rows.ndim - 1).reshape(values.shape)


def sub_roll(values, shift):
    rows = flat(values)
    return pltpu.roll(rows, shift % 8, 1).reshape(values.shape)


def lane_roll(values, shift):
    rows = flat(values)
    return pltpu.roll(rows, shift % 128, 2).reshape(values.shape)


class Level:
    def __init__(self, depth, refs):
        self.depth = depth
        self.scale = 0.5 * 0.25**depth
        self.mob, self.src, self.az, self.ay, self.ax, self.inv, self.val, self.smo, self.err, self.rem = refs

    def field_one(self, shape):
        if self.depth == 0:
            return sub_iota(shape) >= 4
        if self.depth == 1:
            return (sub_iota(shape) // 2) % 2 == 1
        if self.depth == 2:
            return sub_iota(shape) % 2 == 1
        return lane_iota(shape) >= 64

    def x_side(self, values, step):
        if self.depth <= 2:
            rolled = lane_roll(values, -step)
            if self.depth == 2:
                return rolled
            if self.depth == 0:
                other = sub_take(rolled, lambda s: (s // 4) * 4 + (s + step + 4) % 4)
            else:
                other = sub_take(rolled, lambda s: s + 1 - 2 * (s % 2))
            edge = 127 if step == 1 else 0
            return jnp.where(lane_iota(values.shape) == edge, other, rolled)
        wide = 2 ** (self.depth - 3)
        return lane_take(values, lambda s, l: (l // 64) * 64 + (l + step * wide + 64) % 64)

    def y_side(self, values, step):
        rows = {1: 4, 2: 2}.get(self.depth, 1)
        count = values.shape[1]
        if count == 1:
            other = values
        elif step == 1:
            other = jnp.concatenate([values[:, 1:], values[:, :1]], axis=1)
        else:
            other = jnp.concatenate([values[:, -1:], values[:, :-1]], axis=1)
        place = sub_iota(values.shape)
        edge = place < rows if step == 1 else place >= 8 - rows
        return sub_roll(jnp.where(edge, other, values), -step * rows)

    def coefficients(self, at, count, mask=None):
        here = self.mob[pl.ds(at, count)]
        up = self.scale * (here + self.mob[pl.ds(at + 1, count)])
        down = self.scale * (here + self.mob[pl.ds(at - 1, count)])
        right = self.scale * (here + self.y_side(here, 1))
        ahead = self.scale * (here + self.x_side(here, 1))
        diagonal = up + down + right + self.y_side(right, -1) + ahead + self.x_side(ahead, -1)
        self.az[pl.ds(at, count)] = up
        self.ay[pl.ds(at, count)] = right
        self.ax[pl.ds(at, count)] = ahead
        return self.masked_inverse(diagonal, mask)

    def masked_inverse(self, diagonal, mask):
        if mask is None:
            return 1.0 / diagonal
        return mask / (diagonal + (1.0 - mask))

    def operate(self, ref, at, count):
        here = ref[pl.ds(at, count)]
        total = self.az[pl.ds(at, count)] * (here - ref[pl.ds(at + 1, count)])
        total = total + self.az[pl.ds(at - 1, count)] * (here - ref[pl.ds(at - 1, count)])
        flux = self.ay[pl.ds(at, count)] * (here - self.y_side(here, 1))
        total = total + (flux - self.y_side(flux, -1))
        flux = self.ax[pl.ds(at, count)] * (here - self.x_side(here, 1))
        return here, total + (flux - self.x_side(flux, -1))

    def start(self, at, count):
        self.val[pl.ds(at, count)] = self.src[pl.ds(at, count)] * self.inv[pl.ds(at, count)] * (1.0 / MID)

    def smooth(self, at, count):
        here, applied = self.operate(self.val, at, count)
        rest = self.src[pl.ds(at, count)] - applied
        second = here + C1 * here + C2 * (self.inv[pl.ds(at, count)] * rest)
        self.smo[pl.ds(at, count)] = jnp.where(self.field_one(here.shape), here, second)

    def remainder(self, at, count):
        _, applied = self.operate(self.smo, at, count)
        return self.src[pl.ds(at, count)] - applied

    def correct(self, at, count):
        _, applied = self.operate(self.val, at, count)
        rest = self.src[pl.ds(at, count)] - applied
        self.rem[pl.ds(at, count)] = rest
        self.err[pl.ds(at, count)] = rest * self.inv[pl.ds(at, count)] * (1.0 / MID)

    def finish(self, at, count):
        here, applied = self.operate(self.err, at, count)
        rest = self.rem[pl.ds(at, count)] - applied
        second = C1 * here + C2 * (self.inv[pl.ds(at, count)] * rest)
        base = self.val[pl.ds(at, count)] + here
        return jnp.where(self.field_one(here.shape), base + second, base)


class Finest(Level):
    def coefficients(self, plane, low, count, mask):
        here = self.mob[plane + 1, pl.ds(low, count + 2)]
        mid = here[1:-1]
        up = self.scale * (mid + self.mob[plane + 2, pl.ds(low + 1, count)])
        down = self.scale * (mid + self.mob[plane, pl.ds(low + 1, count)])
        right = self.scale * (here[:-1] + here[1:])
        ahead = self.scale * (mid + self.x_side(mid, 1))
        diagonal = up + down + right[1:] + right[:-1] + ahead + self.x_side(ahead, -1)
        self.az[plane, pl.ds(low, count)] = up
        self.ay[plane, pl.ds(low, count)] = right[1:]
        self.ax[plane, pl.ds(low, count)] = ahead
        self.inv[plane, pl.ds(low, count)] = self.masked_inverse(diagonal, mask)

    def operate(self, ref, plane, low, count):
        wide = ref[plane, pl.ds(low - 1, count + 2)]
        here = wide[1:-1]
        part = pl.ds(low, count)
        total = self.az[plane, part] * (here - ref[plane + 1, part])
        total = total + self.az[plane - 1, part] * (here - ref[plane - 1, part])
        flux = self.ay[plane, pl.ds(low - 1, count + 1)] * (wide[:-1] - wide[1:])
        total = total + (flux[1:] - flux[:-1])
        flux = self.ax[plane, part] * (here - self.x_side(here, 1))
        return here, total + (flux - self.x_side(flux, -1))

    def start(self, plane, low, count):
        part = pl.ds(low, count)
        self.val[plane, part] = self.src[plane, part] * self.inv[plane, part] * (1.0 / MID)

    def smooth(self, plane, low, count):
        part = pl.ds(low, count)
        here, applied = self.operate(self.val, plane, low, count)
        rest = self.src[plane, part] - applied
        second = here + C1 * here + C2 * (self.inv[plane, part] * rest)
        self.smo[plane, part] = jnp.where(self.field_one(here.shape), here, second)

    def remainder(self, plane, low, count):
        _, applied = self.operate(self.smo, plane, low, count)
        return self.src[plane, pl.ds(low, count)] - applied

    def correct(self, plane, low, count):
        part = pl.ds(low, count)
        _, applied = self.operate(self.val, plane, low, count)
        rest = self.src[plane, part] - applied
        self.rem[plane, part] = rest
        self.err[plane, part] = rest * self.inv[plane, part] * (1.0 / MID)

    def finish(self, plane, low, count):
        part = pl.ds(low, count)
        here, applied = self.operate(self.err, plane, low, count)
        rest = self.rem[plane, part] - applied
        second = C1 * here + C2 * (self.inv[plane, part] * rest)
        base = self.val[plane, part] + here
        return jnp.where(self.field_one(here.shape), base + second, base)


def halves(values):
    return lane_take(values + lane_roll(values, -1), lambda s, l: (2 * l) % 128)


def restrict_0(planes):
    count = planes.shape[0] // 4
    four = planes.reshape((count, 4) + planes.shape[1:])
    out = []
    for pair in (0, 2):
        got = halves(four[:, pair] + four[:, pair + 1])
        left = sub_take(got, lambda s: ((s // 2) % 2) * 4 + 2 * (s % 2))
        right = sub_take(got, lambda s: ((s // 2) % 2) * 4 + 2 * (s % 2) + 1)
        out.append(jnp.where(lane_iota(got.shape) < 64, left, right))
    return 0.125 * jnp.where(sub_iota(out[0].shape) < 4, out[0], out[1])


def restrict_1(planes):
    got = halves(planes + sub_roll(planes, 4))
    left = sub_take(got, lambda s: (s % 2) * 2)
    right = sub_take(got, lambda s: (s % 2) * 2 + 1)
    both = jnp.where(lane_iota(got.shape) < 64, left, right)
    row = sub_iota(both[:, 0].shape) // 2
    out = jnp.where(row == 0, both[:, 0], both[:, 1])
    out = jnp.where(row == 2, both[:, 2], out)
    return 0.125 * jnp.where(row == 3, both[:, 3], out)


def restrict_2(planes):
    got = halves(planes + sub_roll(planes, -2))
    left = sub_take(got, lambda s: (4 * s) % 8)
    right = sub_take(got, lambda s: (4 * s + 1) % 8)
    return 0.125 * jnp.where(lane_iota(got.shape) < 64, left, right)


def restrict_whole(planes, depth):
    wide = 2 ** (depth - 3)
    got = planes + lane_take(planes, lambda s, l: l + wide - 2 * wide * ((l // wide) % 2))
    got = sub_take(got + sub_roll(got, -1), lambda s: (2 * s) % 8)
    count = got.shape[1]
    if count == 1:
        return 0.125 * got
    pairs = got.reshape((got.shape[0], count // 2, 2, 8, 128))
    low = sub_iota(pairs[:, :, 0].shape) < 4
    return 0.125 * jnp.where(low, pairs[:, :, 0], pairs[:, :, 1])


def pair_sum(planes):
    pairs = planes.reshape((planes.shape[0] // 2, 2) + planes.shape[1:])
    return pairs[:, 0] + pairs[:, 1]


def twice(planes):
    shape = (planes.shape[0], 2) + planes.shape[1:]
    return jnp.broadcast_to(planes[:, None], shape).reshape((2 * planes.shape[0],) + planes.shape[1:])


def prolong_whole(coarse, depth):
    if depth == 5:
        return twice(sub_take(coarse, lambda s: s // 2))
    low = sub_take(coarse, lambda s: s // 2)
    high = sub_take(coarse, lambda s: 4 + s // 2)
    both = jnp.stack([low, high], axis=2)
    return twice(both.reshape((coarse.shape[0], 2 * coarse.shape[1], 8, 128)))


def loop(count, body):
    def step(i, carry):
        body(i)
        return carry

    lax.fori_loop(0, count, step, 0)


def kernel(rhs, cot, phase, out_a, out_b, *scratch):
    scratch = list(scratch)

    def take(count):
        got = scratch[:count]
        del scratch[:count]
        return got

    zero = Finest(0, take(10))
    one, two = Level(1, take(10)), Level(2, take(10))
    whole = [Level(depth, take(10)) for depth in range(3, 7)]
    answers = take(5)
    phases, staged, rows_m, rows_s = take(4)
    in_sem, out_sem, near_send, near_recv, far_send, far_recv = take(6)
    gy, gz = lax.axis_index("gy"), lax.axis_index("gz")

    def to_z(step):
        return {"gz": lax.rem(gz + step + RING, RING)}

    def to_y(step):
        return {"gy": lax.rem(gy + step + RING, RING)}

    def to(dy, dz):
        return {"gy": lax.rem(gy + dy + RING, RING), "gz": lax.rem(gz + dz + RING, RING)}

    loads = []
    for group, (src, dst, first) in enumerate(((phase, phases, 0), (rhs, zero.src, 0), (cot, zero.src, 4))):
        edge = 3 if group == 0 else 2
        parts = []
        for part in range(4):
            copy = pltpu.make_async_copy(
                src.at[:, :, pl.ds(128 * part, 128)],
                dst.at[pl.ds(edge, 16), pl.ds(edge, 16), first + part],
                in_sem.at[4 * group + part],
            )
            copy.start()
            parts.append(copy)
        loads.append(parts)

    barrier = pltpu.get_barrier_semaphore()
    for dy, dz in ((1, 1), (1, -1), (-1, 1), (-1, -1)):
        pl.semaphore_signal(barrier, inc=1, device_id=to(dy, dz), device_id_type=MESH)

    def greet(i):
        pl.semaphore_signal(barrier, inc=1, device_id=to_z(i + 1), device_id_type=MESH)
        pl.semaphore_signal(barrier, inc=1, device_id=to_y(i + 1), device_id_type=MESH)

    loop(RING - 1, greet)

    for level in whole:
        count = level.val.shape[0]
        blank = jnp.zeros((1,) + level.val.shape[1:], F32)
        for ref in (level.mob, level.val, level.smo, level.err):
            ref[pl.ds(0, 1)] = blank
            ref[pl.ds(count - 1, 1)] = blank
    for level in whole:
        level.az[pl.ds(0, 1)] = jnp.zeros((1,) + level.val.shape[1:], F32)
    for end in (0, 34):
        answers[2][pl.ds(end, 2)] = jnp.zeros((2, 4, 8, 128), F32)

    def inside(position, extent):
        ok = jnp.logical_and(position >= 0, position < extent)
        return jnp.where(ok, 1.0, 0.0).astype(F32)

    def mobility_of(values, mask):
        found = jnp.where(values == 1, HEAVY, LIGHT).astype(F32) * mask
        return sub_take(found, lambda s: s % 4)

    for copy in loads[0]:
        copy.wait()

    def own_mobility(i):
        total = None
        for plane in (0, 1):
            at = 3 + 2 * i + plane
            found = mobility_of(phases[at, pl.ds(3, 16)], 1.0)
            zero.mob[at, pl.ds(3, 16)] = found
            total = found if total is None else total + found
        one.mob[4 + i, pl.ds(2, 4)] = restrict_0(total)

    loop(8, own_mobility)
    two.mob[pl.ds(4, 4), 1] = restrict_1(pair_sum(one.mob[pl.ds(4, 8), pl.ds(2, 4)]))
    rows_m[...] = restrict_2(pair_sum(two.mob[pl.ds(4, 4), 1]))
    for copy in loads[1] + loads[2]:
        copy.wait()

    pl.semaphore_wait(barrier, 4 + 2 * (RING - 1))

    def edges(step, low, size, width):
        if step == 0:
            return low, low, size
        if step == 1:
            return low + size - width, low - width, width
        return low, low + size, width

    def exchange(slot, ref, z_geometry, y_geometry, rows=None):
        copies = []
        for number, (dy, dz) in enumerate(AROUND):
            z_from, z_to, z_count = edges(dz, *z_geometry)
            y_from, y_to, y_count = edges(dy, *y_geometry)
            src = (pl.ds(z_from, z_count), pl.ds(y_from, y_count))
            dst = (pl.ds(z_to, z_count), pl.ds(y_to, y_count))
            if rows is not None:
                src, dst = src + (pl.ds(0, rows),), dst + (pl.ds(0, rows),)
            copy = pltpu.make_async_remote_copy(
                src_ref=ref.at[src],
                dst_ref=ref.at[dst],
                send_sem=near_send.at[slot, number],
                recv_sem=near_recv.at[slot, number],
                device_id=to(dy, dz),
                device_id_type=MESH,
            )
            copy.start()
            copies.append(copy)
        return copies

    def landed(copies):
        for copy in copies:
            copy.wait_recv()

    def place(ref):
        return ref.at[pl.ds(2 * gz + 1, 2), gy // 4, pl.ds(2 * lax.rem(gy, 4), 2)]

    def gather_z(slot, rows, ref):
        own = pltpu.make_async_copy(rows.at[pl.ds(0, 2), pl.ds(0, 2)], place(ref), far_send.at[slot, 2])
        own.start()

        def send(i):
            pltpu.make_async_remote_copy(
                src_ref=rows.at[pl.ds(0, 2), pl.ds(0, 2)],
                dst_ref=place(ref),
                send_sem=far_send.at[slot, 0],
                recv_sem=far_recv.at[slot, 0],
                device_id=to_z(i + 1),
                device_id_type=MESH,
            ).start()

        loop(RING - 1, send)
        return own

    def settle(ref, semaphore, planes):
        part = ref.at[pl.ds(1, planes), 0, pl.ds(0, 2)]
        pltpu.make_async_copy(part, part, semaphore).wait()

    def gather_y(slot, ref, own):
        own.wait()
        settle(ref, far_recv.at[slot, 0], 2 * (RING - 1))
        part = ref.at[pl.ds(1, 32), gy // 4, pl.ds(2 * lax.rem(gy, 4), 2)]

        def send(i):
            pltpu.make_async_remote_copy(
                src_ref=part,
                dst_ref=part,
                send_sem=far_send.at[slot, 1],
                recv_sem=far_recv.at[slot, 1],
                device_id=to_y(i + 1),
                device_id_type=MESH,
            ).start()

        loop(RING - 1, send)

    def drain(ref, semaphore):
        part = ref.at[pl.ds(1, 30)]
        pltpu.make_async_copy(part, part, semaphore).wait()

    sent = []
    phase_halo = exchange(0, phases, (3, 16, 3), (3, 16, 3), 4)
    source_halo = exchange(1, zero.src, (2, 16, 2), (2, 16, 2))
    own_m = gather_z(0, rows_m, whole[0].mob)
    mob_one = exchange(2, one.mob, (4, 8, 4), (2, 4, 2))
    mob_two = exchange(3, two.mob, (4, 4, 4), (1, 1, 1))
    sent += phase_halo + source_halo + mob_one + mob_two

    def z_mask(plane_at, depth, first):
        block = 16 >> depth
        return inside(gz * block + plane_at - first, 256 >> depth)

    landed(phase_halo)

    def outer_mobility(i):
        at = jnp.where(i < 3, i, i + 16)
        mask = z_mask(at, 0, 3)
        zero.mob[at, pl.ds(0, 22)] = mobility_of(phases[at, pl.ds(0, 22)], mask)

    loop(6, outer_mobility)

    def side_mobility(i):
        for first in (0, 19):
            zero.mob[3 + i, pl.ds(first, 3)] = mobility_of(phases[3 + i, pl.ds(first, 3)], 1.0)

    loop(16, side_mobility)

    def coefficients_zero(i):
        for low in (0, 10):
            zero.coefficients(i, low, 10, z_mask(i, 0, 2))

    loop(20, coefficients_zero)
    landed(source_halo)

    def start_zero(i):
        zero.start(i, 0, 20)

    loop(20, start_zero)

    def smooth_zero(i):
        for low in (1, 10):
            zero.smooth(i + 1, low, 9)

    loop(18, smooth_zero)

    for at in (0, 19):
        zero.smo[at] = zero.val[at]

    def ring_zero(i):
        for at in (0, 19):
            zero.smo[i + 1, at] = zero.val[i + 1, at]

    loop(18, ring_zero)

    def remainder_zero(i):
        for half in (0, 1):
            low = 2 + 8 * half
            total = zero.remainder(2 + 2 * i, low, 8) + zero.remainder(3 + 2 * i, low, 8)
            one.src[4 + i, pl.ds(2 + 2 * half, 2)] = restrict_0(total)

    loop(8, remainder_zero)
    source_one = exchange(4, one.src, (4, 8, 3), (2, 4, 2))
    sent += source_one

    gather_y(0, whole[0].mob, own_m)
    landed(mob_one)
    landed(mob_two)

    def fix_mobility(level, planes, depth):
        for at in range(planes):
            level.mob[at] = level.mob[at] * z_mask(at, depth, planes)
            last = level.mob.shape[0] - 1 - at
            level.mob[last] = level.mob[last] * z_mask(last, depth, planes)

    fix_mobility(one, 4, 1)
    fix_mobility(two, 4, 2)

    def masks(at, count, depth, first):
        return jnp.stack([jnp.full((1, 8, 128), z_mask(at + j, depth, first), F32) for j in range(count)])

    def coefficients_one(i):
        at = 1 + 2 * i
        one.inv[pl.ds(at, 2)] = one.coefficients(at, 2, masks(at, 2, 1, 4))

    loop(7, coefficients_one)

    def coefficients_two(i):
        at = 1 + 2 * i
        found = two.coefficients(at, 2, masks(at, 2, 2, 4))
        two.rem[pl.ds(at, 2)] = found

    loop(5, coefficients_two)
    two.az[0] = two.scale * (two.mob[0] + two.mob[1])
    two.inv[pl.ds(4, 4), 1] = two.rem[pl.ds(4, 4), 1]
    inverse_two = exchange(5, two.inv, (4, 4, 4), (1, 1, 1))
    sent += inverse_two

    landed(source_one)

    def start_one(i):
        one.start(1 + 2 * i, 2)

    loop(7, start_one)

    def smooth_one(i):
        one.smooth(2 + 2 * i, 2)

    loop(6, smooth_one)
    for at in (1, 14):
        one.smo[at] = one.val[at]

    def remainder_one(i):
        rest = one.remainder(4 + 2 * i, 2)[:, 2:6]
        two.src[pl.ds(4 + i, 1), 1] = restrict_1(pair_sum(rest))[0:1]

    loop(4, remainder_one)
    source_two = exchange(6, two.src, (4, 4, 4), (1, 1, 1))
    sent += source_two

    landed(inverse_two)
    for at in (0, 1, 2, 3, 8, 9, 10, 11):
        two.inv[at] = two.inv[at] * z_mask(at, 2, 4)
    landed(source_two)
    for at in (0, 4, 8):
        two.start(at, 4)
    two.smooth(2, 4)
    two.smooth(6, 4)
    for at in (0, 1, 10, 11):
        two.smo[at] = two.val[at]
    rows_s[...] = restrict_2(pair_sum(two.remainder(4, 4)[:, 1]))
    own_s = gather_z(1, rows_s, whole[0].src)

    drain(whole[0].mob, far_recv.at[0, 1])

    block = (4, 8, 8, 4)
    steps = (8, 2, 1, 1)
    for number, level in enumerate(whole):
        size = block[number]
        if number > 0:
            finer = whole[number - 1]

            def coarsen(i, finer=finer, level=level, size=size, number=number):
                total = pair_sum(finer.mob[pl.ds(1 + 2 * size * i, 2 * size)])
                level.mob[pl.ds(1 + size * i, size)] = restrict_whole(total, number + 2)

            loop(steps[number], coarsen)

        level.az[pl.ds(0, 1)] = level.scale * level.mob[pl.ds(1, 1)]

        def coefficients(i, level=level, size=size):
            at = 1 + size * i
            level.inv[pl.ds(at, size)] = level.coefficients(at, size)

        loop(steps[number], coefficients)

    gather_y(1, whole[0].src, own_s)
    drain(whole[0].src, far_recv.at[1, 1])

    for number, level in enumerate(whole[:-1]):
        size = block[number]
        coarser = whole[number + 1]

        def start(i, level=level, size=size):
            level.start(1 + size * i, size)

        def smooth(i, level=level, size=size):
            level.smooth(1 + size * i, size)

        def lower(i, level=level, size=size, coarser=coarser, number=number):
            rest = pair_sum(level.remainder(1 + size * i, size))
            coarser.src[pl.ds(1 + (size // 2) * i, size // 2)] = restrict_whole(rest, number + 3)

        loop(steps[number], start)
        loop(steps[number], smooth)
        loop(steps[number], lower)

    last = whole[-1]
    last.start(1, 4)
    iterate = last.val[pl.ds(1, 4)]
    direction = iterate
    factor = FIRST
    for _ in range(3):
        _, applied = last.operate(last.val, 1, 4)
        following = 1.0 / (2.0 * RATIO - factor)
        rest = last.src[pl.ds(1, 4)] - applied
        direction = (following * factor) * direction + (2.0 * following / HALF) * (last.inv[pl.ds(1, 4)] * rest)
        iterate = iterate + direction
        last.val[pl.ds(1, 4)] = iterate
        factor = following
    coarse, offset = last.val, 1

    for number in (2, 1, 0):
        level = whole[number]
        size = block[number]
        target, shift = ((answers[2], 2), (answers[3], 0), (answers[4], 0))[number]

        def add(i, level=level, size=size, coarse=coarse, offset=offset, number=number):
            part = coarse[pl.ds(offset + (size // 2) * i, size // 2)]
            at = 1 + size * i
            level.val[pl.ds(at, size)] = level.smo[pl.ds(at, size)] + prolong_whole(part, number + 3)

        def correct(i, level=level, size=size):
            level.correct(1 + size * i, size)

        def finish(i, level=level, size=size, target=target, shift=shift):
            target[pl.ds(shift + size * i, size)] = level.finish(1 + size * i, size)

        loop(steps[number], add)
        loop(steps[number], correct)
        loop(steps[number], finish)
        coarse, offset = target, shift

    for pair in range(6):
        parts = []
        for tile in range(3):
            row = 2 * lax.rem(gy - 1 + tile + RING, RING)
            found = answers[2][2 * gz + pair, row // 8]
            found = sub_take(found, lambda s, row=row: lax.rem(row, 8) + s // 4)
            parts.append(lane_take(found, lambda s, l: (s % 2) * 64 + l // 2))
        found = jnp.stack(parts)
        for plane in (2 * pair, 2 * pair + 1):
            two.val[plane] = two.smo[plane] + found
    for at in (1, 6):
        two.correct(at, 5)
    for at in (2, 6):
        answers[1][pl.ds(at, 4)] = two.finish(at, 4)

    def add_one(i):
        for half in (0, 1):
            plane = 1 + 2 * i + half
            parts = []
            for tile in range(8):
                at = tile + 2
                found = sub_take(answers[1][(plane + 4) // 2, at // 4], lambda s, at=at: (at % 4) * 2 + (s // 2) % 2)
                parts.append(lane_take(found, lambda s, l: 64 * (s % 2) + l // 2))
            one.val[plane] = one.smo[plane] + jnp.stack(parts)

    loop(7, add_one)

    def correct_one(i):
        one.correct(2 + 2 * i, 2)

    loop(6, correct_one)

    def finish_one(i):
        answers[0][pl.ds(3 + 2 * i, 2)] = one.finish(3 + 2 * i, 2)

    loop(5, finish_one)

    def add_zero(i):
        parts = []
        for pair in range(10):
            at = pair + 3
            found = sub_take(
                answers[0][i + 3, at // 2],
                lambda s, at=at: (at % 2) * 4 + (s // 4) * 2 + (s % 4) // 2,
            )
            found = lane_take(found, lambda s, l: 64 * (s % 2) + l // 2)
            parts += [found, found]
        added = jnp.stack(parts)
        for plane in (0, 1):
            zero.val[2 * i + plane] = zero.smo[2 * i + plane] + added

    loop(10, add_zero)

    def correct_zero(i):
        for low in (1, 10):
            zero.correct(i + 1, low, 9)

    loop(18, correct_zero)

    def finish_zero(i):
        for low in (2, 10):
            staged[i, pl.ds(low - 2, 8)] = zero.finish(i + 2, low, 8)

    loop(16, finish_zero)

    stores = []
    for group, dst in enumerate((out_a, out_b)):
        for part in range(4):
            copy = pltpu.make_async_copy(
                staged.at[:, :, 4 * group + part], dst.at[:, :, pl.ds(128 * part, 128)], out_sem.at[4 * group + part]
            )
            copy.start()
            stores.append(copy)
    for copy in sent:
        copy.wait_send()
    for slot, ref in ((0, whole[0].mob), (1, whole[0].src)):
        settle(ref, far_send.at[slot, 0], 2 * (RING - 1))
        drain(ref, far_send.at[slot, 1])
    for copy in stores:
        copy.wait()


def scratch_shapes():
    shapes = []

    def arrays(planes, tiles, count=10):
        for _ in range(count):
            shapes.append(pltpu.VMEM((planes, tiles, 8, 128), F32))

    arrays(22, 22, 1)
    arrays(20, 20, 9)
    arrays(16, 8)
    arrays(12, 3)
    for planes, tiles in ((34, 4), (18, 2), (10, 1), (6, 1)):
        arrays(planes, tiles)
    arrays(16, 8, 1)
    arrays(12, 3, 1)
    arrays(36, 4, 1)
    arrays(16, 2, 1)
    arrays(8, 1, 1)
    shapes.append(pltpu.VMEM((22, 22, 8, 128), jnp.int32))
    arrays(16, 16, 1)
    shapes.append(pltpu.VMEM((2, 8, 128), F32))
    shapes.append(pltpu.VMEM((2, 8, 128), F32))
    dma = pltpu.SemaphoreType.DMA
    shapes += [dma((12,)), dma((8,)), dma((7, 8)), dma((7, 8)), dma((2, 3)), dma((2, 2))]
    return shapes


def per_device(right_side, cotangent, phase):
    shape = jax.ShapeDtypeStruct(right_side.shape, F32)
    return pl.pallas_call(
        kernel,
        out_shape=(shape, shape),
        in_specs=[pl.BlockSpec(memory_space=pl.ANY)] * 3,
        out_specs=(pl.BlockSpec(memory_space=pl.ANY),) * 2,
        scratch_shapes=scratch_shapes(),
        compiler_params=pltpu.CompilerParams(
            collective_id=0, has_side_effects=True, vmem_limit_bytes=48 * 2**20
        ),
    )(right_side, cotangent, phase)


def solution(mesh):
    spec = P("gz", "gy", None)
    return jax.shard_map(
        per_device, mesh=mesh, in_specs=(spec,) * 3, out_specs=(spec,) * 2, check_vma=False
    )
```

```python
import functools

import jax
import jax.numpy as jnp
from jax import lax
from jax.experimental import pallas as pl
from jax.experimental.pallas import tpu as pltpu
from jax.sharding import PartitionSpec as P

MESH = pl.DeviceIdType.MESH
RING = 16
MID = 1.125
HALF = 0.875
RATIO = MID / HALF
FIRST = 1.0 / RATIO
SECOND = 1.0 / (2.0 * RATIO - FIRST)
C1 = SECOND * FIRST
C2 = 2.0 * SECOND / HALF
LIGHT = 1.0
HEAVY = 1.0 / 8.0
AROUND = tuple((a, b) for a in (-1, 0, 1) for b in (-1, 0, 1) if (a, b) != (0, 0))
F32 = jnp.float32


def flat(values):
    return values.reshape((-1,) + values.shape[-2:])


def sub_iota(shape):
    return lax.broadcasted_iota(jnp.int32, shape, len(shape) - 2)


def lane_iota(shape):
    return lax.broadcasted_iota(jnp.int32, shape, len(shape) - 1)


def sub_take(values, index_of):
    rows = flat(values)
    if rows.shape[0] == 1:
        rows = rows[0]
    index = index_of(sub_iota(rows.shape))
    return jnp.take_along_axis(rows, index, axis=rows.ndim - 2).reshape(values.shape)


def lane_take(values, index_of):
    rows = flat(values)
    if rows.shape[0] == 1:
        rows = rows[0]
    index = index_of(sub_iota(rows.shape), lane_iota(rows.shape))
    return jnp.take_along_axis(rows, index, axis=rows.ndim - 1).reshape(values.shape)


def sub_roll(values, shift):
    rows = flat(values)
    return pltpu.roll(rows, shift % 8, 1).reshape(values.shape)


def lane_roll(values, shift):
    rows = flat(values)
    return pltpu.roll(rows, shift % 128, 2).reshape(values.shape)


class Level:
    def __init__(self, depth, refs):
        self.depth = depth
        self.scale = 0.5 * 0.25**depth
        self.mob, self.src, self.az, self.ay, self.ax, self.bx, self.inv, self.val, self.smo, self.err, self.rem = refs

    def field_one(self, shape):
        if self.depth == 0:
            return sub_iota(shape) >= 4
        if self.depth == 1:
            return (sub_iota(shape) // 2) % 2 == 1
        if self.depth == 2:
            return sub_iota(shape) % 2 == 1
        return lane_iota(shape) >= 64

    def x_side(self, values, step):
        if self.depth <= 2:
            rolled = lane_roll(values, -step)
            if self.depth == 2:
                return rolled
            if self.depth == 0:
                other = sub_take(rolled, lambda s: (s // 4) * 4 + (s + step + 4) % 4)
            else:
                other = sub_take(rolled, lambda s: s + 1 - 2 * (s % 2))
            edge = 127 if step == 1 else 0
            return jnp.where(lane_iota(values.shape) == edge, other, rolled)
        wide = 2 ** (self.depth - 3)
        return lane_take(values, lambda s, l: (l // 64) * 64 + (l + step * wide + 64) % 64)

    def y_side(self, values, step):
        rows = {1: 4, 2: 2}.get(self.depth, 1)
        count = values.shape[1]
        if count == 1:
            other = values
        elif step == 1:
            other = jnp.concatenate([values[:, 1:], values[:, :1]], axis=1)
        else:
            other = jnp.concatenate([values[:, -1:], values[:, :-1]], axis=1)
        place = sub_iota(values.shape)
        edge = place < rows if step == 1 else place >= 8 - rows
        return sub_roll(jnp.where(edge, other, values), -step * rows)

    def coefficients(self, at, count, mask=None):
        here = self.mob[pl.ds(at, count)]
        up = self.scale * (here + self.mob[pl.ds(at + 1, count)])
        down = self.scale * (here + self.mob[pl.ds(at - 1, count)])
        right = self.scale * (here + self.y_side(here, 1))
        ahead = self.scale * (here + self.x_side(here, 1))
        behind = self.scale * (here + self.x_side(here, -1))
        diagonal = up + down + right + self.y_side(right, -1) + ahead + behind
        self.az[pl.ds(at, count)] = up
        self.ay[pl.ds(at, count)] = right
        self.ax[pl.ds(at, count)] = ahead
        self.bx[pl.ds(at, count)] = behind
        return self.masked_inverse(diagonal, mask)

    def masked_inverse(self, diagonal, mask):
        if mask is None:
            return 1.0 / diagonal
        return mask / (diagonal + (1.0 - mask))

    def operate(self, ref, at, count):
        here = ref[pl.ds(at, count)]
        total = self.az[pl.ds(at, count)] * (here - ref[pl.ds(at + 1, count)])
        total = total + self.az[pl.ds(at - 1, count)] * (here - ref[pl.ds(at - 1, count)])
        flux = self.ay[pl.ds(at, count)] * (here - self.y_side(here, 1))
        total = total + (flux - self.y_side(flux, -1))
        total = total + self.ax[pl.ds(at, count)] * (here - self.x_side(here, 1))
        return here, total + self.bx[pl.ds(at, count)] * (here - self.x_side(here, -1))

    def start(self, at, count):
        self.val[pl.ds(at, count)] = self.src[pl.ds(at, count)] * self.inv[pl.ds(at, count)] * (1.0 / MID)

    def smooth(self, at, count):
        here, applied = self.operate(self.val, at, count)
        rest = self.src[pl.ds(at, count)] - applied
        second = here + C1 * here + C2 * (self.inv[pl.ds(at, count)] * rest)
        self.smo[pl.ds(at, count)] = jnp.where(self.field_one(here.shape), here, second)

    def remainder(self, at, count):
        _, applied = self.operate(self.smo, at, count)
        return self.src[pl.ds(at, count)] - applied

    def correct(self, at, count):
        _, applied = self.operate(self.val, at, count)
        rest = self.src[pl.ds(at, count)] - applied
        self.rem[pl.ds(at, count)] = rest
        self.err[pl.ds(at, count)] = rest * self.inv[pl.ds(at, count)] * (1.0 / MID)

    def finish(self, at, count):
        here, applied = self.operate(self.err, at, count)
        rest = self.rem[pl.ds(at, count)] - applied
        second = C1 * here + C2 * (self.inv[pl.ds(at, count)] * rest)
        base = self.val[pl.ds(at, count)] + here
        return jnp.where(self.field_one(here.shape), base + second, base)


class Finest(Level):
    def coefficients(self, plane, low, count, mask):
        here = self.mob[plane + 1, pl.ds(low, count + 2)]
        mid = here[1:-1]
        up = self.scale * (mid + self.mob[plane + 2, pl.ds(low + 1, count)])
        down = self.scale * (mid + self.mob[plane, pl.ds(low + 1, count)])
        right = self.scale * (here[:-1] + here[1:])
        ahead = self.scale * (mid + self.x_side(mid, 1))
        behind = self.scale * (mid + self.x_side(mid, -1))
        diagonal = up + down + right[1:] + right[:-1] + ahead + behind
        self.az[plane, pl.ds(low, count)] = up
        self.ay[plane, pl.ds(low, count)] = right[1:]
        self.ax[plane, pl.ds(low, count)] = ahead
        self.bx[plane, pl.ds(low, count)] = behind
        self.inv[plane, pl.ds(low, count)] = self.masked_inverse(diagonal, mask)

    def operate(self, ref, plane, low, count):
        wide = ref[plane, pl.ds(low - 1, count + 2)]
        here = wide[1:-1]
        part = pl.ds(low, count)
        total = self.az[plane, part] * (here - ref[plane + 1, part])
        total = total + self.az[plane - 1, part] * (here - ref[plane - 1, part])
        flux = self.ay[plane, pl.ds(low - 1, count + 1)] * (wide[:-1] - wide[1:])
        total = total + (flux[1:] - flux[:-1])
        total = total + self.ax[plane, part] * (here - self.x_side(here, 1))
        return here, total + self.bx[plane, part] * (here - self.x_side(here, -1))

    def start(self, plane, low, count):
        part = pl.ds(low, count)
        self.val[plane, part] = self.src[plane, part] * self.inv[plane, part] * (1.0 / MID)

    def smooth(self, plane, low, count):
        part = pl.ds(low, count)
        here, applied = self.operate(self.val, plane, low, count)
        rest = self.src[plane, part] - applied
        second = here + C1 * here + C2 * (self.inv[plane, part] * rest)
        self.smo[plane, part] = jnp.where(self.field_one(here.shape), here, second)

    def remainder(self, plane, low, count):
        _, applied = self.operate(self.smo, plane, low, count)
        return self.src[plane, pl.ds(low, count)] - applied

    def correct(self, plane, low, count):
        part = pl.ds(low, count)
        _, applied = self.operate(self.val, plane, low, count)
        rest = self.src[plane, part] - applied
        self.rem[plane, part] = rest
        self.err[plane, part] = rest * self.inv[plane, part] * (1.0 / MID)

    def finish(self, plane, low, count):
        part = pl.ds(low, count)
        here, applied = self.operate(self.err, plane, low, count)
        rest = self.rem[plane, part] - applied
        second = C1 * here + C2 * (self.inv[plane, part] * rest)
        base = self.val[plane, part] + here
        return jnp.where(self.field_one(here.shape), base + second, base)


def halves(values):
    return lane_take(values, lambda s, l: (2 * l) % 128) + lane_take(values, lambda s, l: (2 * l + 1) % 128)


def restrict_0(planes):
    count = planes.shape[0] // 4
    four = planes.reshape((count, 4) + planes.shape[1:])
    out = []
    for pair in (0, 2):
        got = halves(four[:, pair] + four[:, pair + 1])
        left = sub_take(got, lambda s: ((s // 2) % 2) * 4 + 2 * (s % 2))
        right = sub_take(got, lambda s: ((s // 2) % 2) * 4 + 2 * (s % 2) + 1)
        out.append(jnp.where(lane_iota(got.shape) < 64, left, right))
    return 0.125 * jnp.where(sub_iota(out[0].shape) < 4, out[0], out[1])


def restrict_1(planes):
    got = halves(planes + sub_roll(planes, 4))
    left = sub_take(got, lambda s: (s % 2) * 2)
    right = sub_take(got, lambda s: (s % 2) * 2 + 1)
    both = jnp.where(lane_iota(got.shape) < 64, left, right)
    row = sub_iota(both[:, 0].shape) // 2
    out = jnp.where(row == 0, both[:, 0], both[:, 1])
    out = jnp.where(row == 2, both[:, 2], out)
    return 0.125 * jnp.where(row == 3, both[:, 3], out)


def restrict_2(planes):
    got = halves(planes + sub_roll(planes, -2))
    left = sub_take(got, lambda s: (4 * s) % 8)
    right = sub_take(got, lambda s: (4 * s + 1) % 8)
    return 0.125 * jnp.where(lane_iota(got.shape) < 64, left, right)


def restrict_whole(planes, depth):
    wide = 2 ** (depth - 3)
    got = planes + lane_take(planes, lambda s, l: l + wide - 2 * wide * ((l // wide) % 2))
    got = sub_take(got + sub_roll(got, -1), lambda s: (2 * s) % 8)
    count = got.shape[1]
    if count == 1:
        return 0.125 * got
    pairs = got.reshape((got.shape[0], count // 2, 2, 8, 128))
    low = sub_iota(pairs[:, :, 0].shape) < 4
    return 0.125 * jnp.where(low, pairs[:, :, 0], pairs[:, :, 1])


def pair_sum(planes):
    pairs = planes.reshape((planes.shape[0] // 2, 2) + planes.shape[1:])
    return pairs[:, 0] + pairs[:, 1]


def twice(planes):
    shape = (planes.shape[0], 2) + planes.shape[1:]
    return jnp.broadcast_to(planes[:, None], shape).reshape((2 * planes.shape[0],) + planes.shape[1:])


def prolong_whole(coarse, depth):
    if depth == 5:
        return twice(sub_take(coarse, lambda s: s // 2))
    low = sub_take(coarse, lambda s: s // 2)
    high = sub_take(coarse, lambda s: 4 + s // 2)
    both = jnp.stack([low, high], axis=2)
    return twice(both.reshape((coarse.shape[0], 2 * coarse.shape[1], 8, 128)))


def loop(count, body, unroll=1):
    def step(i, carry):
        body(i)
        return carry

    lax.fori_loop(0, count, step, 0, unroll=unroll)


def kernel(rhs, cot, phase, out_a, out_b, *scratch):
    scratch = list(scratch)

    def take(count):
        got = scratch[:count]
        del scratch[:count]
        return got

    zero = Finest(0, take(11))
    one, two = Level(1, take(11)), Level(2, take(11))
    whole = [Level(depth, take(11)) for depth in range(3, 7)]
    answers = take(5)
    phases, staged, rows_m, rows_s = take(4)
    in_sem, out_sem, near_send, near_recv, far_send, far_recv, known = take(7)
    gy, gz = lax.axis_index("gy"), lax.axis_index("gz")

    def to_z(step):
        return {"gz": lax.rem(gz + step + RING, RING)}

    def to_y(step):
        return {"gy": lax.rem(gy + step + RING, RING)}

    def to(dy, dz):
        return {"gy": lax.rem(gy + dy + RING, RING), "gz": lax.rem(gz + dz + RING, RING)}

    loads = []
    for group, (src, dst, first) in enumerate(((phase, phases, 0), (rhs, zero.src, 0), (cot, zero.src, 4))):
        edge = 3 if group == 0 else 2
        parts = []
        for part in range(4):
            copy = pltpu.make_async_copy(
                src.at[:, :, pl.ds(128 * part, 128)],
                dst.at[pl.ds(edge, 16), pl.ds(edge, 16), first + part],
                in_sem.at[4 * group + part],
            )
            copy.start()
            parts.append(copy)
        loads.append(parts)

    barrier = pltpu.get_barrier_semaphore()
    for dy, dz in AROUND:
        pl.semaphore_signal(barrier, inc=1, device_id=to(dy, dz), device_id_type=MESH)

    for level in whole:
        count = level.val.shape[0]
        blank = jnp.zeros((1,) + level.val.shape[1:], F32)
        for ref in (level.mob, level.val, level.smo, level.err):
            ref[pl.ds(0, 1)] = blank
            ref[pl.ds(count - 1, 1)] = blank
    for level in whole:
        level.az[pl.ds(0, 1)] = jnp.zeros((1,) + level.val.shape[1:], F32)
    for end in (0, 34):
        answers[2][pl.ds(end, 2)] = jnp.zeros((2, 4, 8, 128), F32)

    def inside(position, extent):
        ok = jnp.logical_and(position >= 0, position < extent)
        return jnp.where(ok, 1.0, 0.0).astype(F32)

    def mobility_of(values, mask):
        found = jnp.where(values == 1, HEAVY, LIGHT).astype(F32) * mask
        return sub_take(found, lambda s: s % 4)

    for copy in loads[0]:
        copy.wait()

    def own_mobility(i):
        total = None
        for plane in (0, 1):
            at = 3 + 2 * i + plane
            found = mobility_of(phases[at, pl.ds(3, 16)], 1.0)
            zero.mob[at, pl.ds(3, 16)] = found
            total = found if total is None else total + found
        one.mob[4 + i, pl.ds(2, 4)] = restrict_0(total)

    loop(8, own_mobility, 2)
    two.mob[pl.ds(4, 4), 1] = restrict_1(pair_sum(one.mob[pl.ds(4, 8), pl.ds(2, 4)]))
    rows_m[...] = restrict_2(pair_sum(two.mob[pl.ds(4, 4), 1]))
    for copy in loads[1] + loads[2]:
        copy.wait()

    pl.semaphore_wait(barrier, len(AROUND))

    def tell(number):
        away = 2**number
        for device in (to_z(away), to_z(-away), to_y(away), to_y(-away)):
            pl.semaphore_signal(known.at[number], inc=1, device_id=device, device_id_type=MESH)

    tell(0)

    def edges(step, low, size, width):
        if step == 0:
            return low, low, size
        if step == 1:
            return low + size - width, low - width, width
        return low, low + size, width

    def exchange(slot, ref, z_geometry, y_geometry, rows=None):
        copies = []
        for number, (dy, dz) in enumerate(AROUND):
            z_from, z_to, z_count = edges(dz, *z_geometry)
            y_from, y_to, y_count = edges(dy, *y_geometry)
            src = (pl.ds(z_from, z_count), pl.ds(y_from, y_count))
            dst = (pl.ds(z_to, z_count), pl.ds(y_to, y_count))
            if rows is not None:
                src, dst = src + (pl.ds(0, rows),), dst + (pl.ds(0, rows),)
            copy = pltpu.make_async_remote_copy(
                src_ref=ref.at[src],
                dst_ref=ref.at[dst],
                send_sem=near_send.at[slot, number],
                recv_sem=near_recv.at[slot, number],
                device_id=to(dy, dz),
                device_id_type=MESH,
            )
            copy.start()
            copies.append(copy)
        return copies

    def landed(copies):
        for copy in copies:
            copy.wait_recv()

    def place(ref):
        return ref.at[pl.ds(2 * gz + 1, 2), gy // 4, pl.ds(2 * lax.rem(gy, 4), 2)]

    def gather_z(slot, rows, ref):
        own = pltpu.make_async_copy(rows.at[pl.ds(0, 2), pl.ds(0, 2)], place(ref), far_send.at[slot, 2])
        own.start()

        def send(i):
            pltpu.make_async_remote_copy(
                src_ref=rows.at[pl.ds(0, 2), pl.ds(0, 2)],
                dst_ref=place(ref),
                send_sem=far_send.at[slot, 0],
                recv_sem=far_recv.at[slot, 0],
                device_id=to_z(i + 1),
                device_id_type=MESH,
            ).start()

        loop(RING - 1, send)
        return own

    def settle(ref, semaphore, planes):
        part = ref.at[pl.ds(1, planes), 0, pl.ds(0, 2)]
        pltpu.make_async_copy(part, part, semaphore).wait()

    def gather_y(slot, ref, own):
        own.wait()
        settle(ref, far_recv.at[slot, 0], 2 * (RING - 1))
        part = ref.at[pl.ds(1, 32), gy // 4, pl.ds(2 * lax.rem(gy, 4), 2)]

        def send(i):
            pltpu.make_async_remote_copy(
                src_ref=part,
                dst_ref=part,
                send_sem=far_send.at[slot, 1],
                recv_sem=far_recv.at[slot, 1],
                device_id=to_y(i + 1),
                device_id_type=MESH,
            ).start()

        loop(RING - 1, send)

    def drain(ref, semaphore):
        part = ref.at[pl.ds(1, 30)]
        pltpu.make_async_copy(part, part, semaphore).wait()

    sent = []
    phase_halo = exchange(0, phases, (3, 16, 3), (3, 16, 3), 4)
    source_halo = exchange(1, zero.src, (2, 16, 2), (2, 16, 2))
    mob_one = exchange(2, one.mob, (4, 8, 4), (2, 4, 2))
    mob_two = exchange(3, two.mob, (4, 4, 4), (1, 1, 1))
    for number in range(3):
        pl.semaphore_wait(known.at[number], 4)
        if number < 2:
            tell(number + 1)
    own_m = gather_z(0, rows_m, whole[0].mob)
    sent += phase_halo + source_halo + mob_one + mob_two

    def z_mask(plane_at, depth, first):
        block = 16 >> depth
        return inside(gz * block + plane_at - first, 256 >> depth)

    landed(phase_halo)

    def outer_mobility(i):
        at = jnp.where(i < 3, i, i + 16)
        mask = z_mask(at, 0, 3)
        zero.mob[at, pl.ds(0, 22)] = mobility_of(phases[at, pl.ds(0, 22)], mask)

    loop(6, outer_mobility, 2)

    def side_mobility(i):
        for first in (0, 19):
            zero.mob[3 + i, pl.ds(first, 3)] = mobility_of(phases[3 + i, pl.ds(first, 3)], 1.0)

    loop(16, side_mobility, 4)

    def coefficients_zero(i):
        for low in (0, 10):
            zero.coefficients(i, low, 10, z_mask(i, 0, 2))

    loop(20, coefficients_zero, 2)
    landed(source_halo)

    def start_zero(i):
        zero.start(i, 0, 20)

    loop(20, start_zero, 2)

    def smooth_zero(i):
        for low in (1, 10):
            zero.smooth(i + 1, low, 9)

    loop(18, smooth_zero, 3)

    for at in (0, 19):
        zero.smo[at] = zero.val[at]

    def ring_zero(i):
        for at in (0, 19):
            zero.smo[i + 1, at] = zero.val[i + 1, at]

    loop(18, ring_zero, 6)

    def remainder_zero(i):
        for half in (0, 1):
            low = 2 + 8 * half
            total = zero.remainder(2 + 2 * i, low, 8) + zero.remainder(3 + 2 * i, low, 8)
            one.src[4 + i, pl.ds(2 + 2 * half, 2)] = restrict_0(total)

    loop(8, remainder_zero, 2)
    source_one = exchange(4, one.src, (4, 8, 3), (2, 4, 2))
    sent += source_one

    gather_y(0, whole[0].mob, own_m)
    landed(mob_one)
    landed(mob_two)

    def fix_mobility(level, planes, depth):
        for at in range(planes):
            level.mob[at] = level.mob[at] * z_mask(at, depth, planes)
            last = level.mob.shape[0] - 1 - at
            level.mob[last] = level.mob[last] * z_mask(last, depth, planes)

    fix_mobility(one, 4, 1)
    fix_mobility(two, 4, 2)

    def masks(at, count, depth, first):
        return jnp.stack([jnp.full((1, 8, 128), z_mask(at + j, depth, first), F32) for j in range(count)])

    def coefficients_one(i):
        at = 1 + 2 * i
        one.inv[pl.ds(at, 2)] = one.coefficients(at, 2, masks(at, 2, 1, 4))

    loop(7, coefficients_one, 7)

    def coefficients_two(i):
        at = 1 + 2 * i
        found = two.coefficients(at, 2, masks(at, 2, 2, 4))
        two.rem[pl.ds(at, 2)] = found

    loop(5, coefficients_two, 5)
    two.az[0] = two.scale * (two.mob[0] + two.mob[1])
    two.inv[pl.ds(4, 4), 1] = two.rem[pl.ds(4, 4), 1]
    inverse_two = exchange(5, two.inv, (4, 4, 4), (1, 1, 1))
    sent += inverse_two

    landed(source_one)

    def start_one(i):
        one.start(1 + 2 * i, 2)

    loop(7, start_one, 7)

    def smooth_one(i):
        one.smooth(2 + 2 * i, 2)

    loop(6, smooth_one, 6)
    for at in (1, 14):
        one.smo[at] = one.val[at]

    def remainder_one(i):
        rest = one.remainder(4 + 2 * i, 2)[:, 2:6]
        two.src[pl.ds(4 + i, 1), 1] = restrict_1(pair_sum(rest))[0:1]

    loop(4, remainder_one, 4)
    source_two = exchange(6, two.src, (4, 4, 4), (1, 1, 1))
    sent += source_two

    landed(inverse_two)
    for at in (0, 1, 2, 3, 8, 9, 10, 11):
        two.inv[at] = two.inv[at] * z_mask(at, 2, 4)
    landed(source_two)
    for at in (0, 4, 8):
        two.start(at, 4)
    two.smooth(2, 4)
    two.smooth(6, 4)
    for at in (0, 1, 10, 11):
        two.smo[at] = two.val[at]
    rows_s[...] = restrict_2(pair_sum(two.remainder(4, 4)[:, 1]))
    own_s = gather_z(1, rows_s, whole[0].src)

    drain(whole[0].mob, far_recv.at[0, 1])

    block = (4, 8, 8, 4)
    steps = (8, 2, 1, 1)
    for number, level in enumerate(whole):
        size = block[number]
        if number > 0:
            finer = whole[number - 1]

            def coarsen(i, finer=finer, level=level, size=size, number=number):
                total = pair_sum(finer.mob[pl.ds(1 + 2 * size * i, 2 * size)])
                level.mob[pl.ds(1 + size * i, size)] = restrict_whole(total, number + 2)

            loop(steps[number], coarsen, steps[number])

        level.az[pl.ds(0, 1)] = level.scale * level.mob[pl.ds(1, 1)]

        def coefficients(i, level=level, size=size):
            at = 1 + size * i
            level.inv[pl.ds(at, size)] = level.coefficients(at, size)

        loop(steps[number], coefficients, steps[number])

    gather_y(1, whole[0].src, own_s)
    drain(whole[0].src, far_recv.at[1, 1])

    for number, level in enumerate(whole[:-1]):
        size = block[number]
        coarser = whole[number + 1]

        def start(i, level=level, size=size):
            level.start(1 + size * i, size)

        def smooth(i, level=level, size=size):
            level.smooth(1 + size * i, size)

        def lower(i, level=level, size=size, coarser=coarser, number=number):
            rest = pair_sum(level.remainder(1 + size * i, size))
            coarser.src[pl.ds(1 + (size // 2) * i, size // 2)] = restrict_whole(rest, number + 3)

        loop(steps[number], start, steps[number])
        loop(steps[number], smooth, steps[number])
        loop(steps[number], lower, steps[number])

    last = whole[-1]
    last.start(1, 4)
    iterate = last.val[pl.ds(1, 4)]
    direction = iterate
    factor = FIRST
    for _ in range(3):
        _, applied = last.operate(last.val, 1, 4)
        following = 1.0 / (2.0 * RATIO - factor)
        rest = last.src[pl.ds(1, 4)] - applied
        direction = (following * factor) * direction + (2.0 * following / HALF) * (last.inv[pl.ds(1, 4)] * rest)
        iterate = iterate + direction
        last.val[pl.ds(1, 4)] = iterate
        factor = following
    coarse, offset = last.val, 1

    for number in (2, 1, 0):
        level = whole[number]
        size = block[number]
        target, shift = ((answers[2], 2), (answers[3], 0), (answers[4], 0))[number]

        def add(i, level=level, size=size, coarse=coarse, offset=offset, number=number):
            part = coarse[pl.ds(offset + (size // 2) * i, size // 2)]
            at = 1 + size * i
            level.val[pl.ds(at, size)] = level.smo[pl.ds(at, size)] + prolong_whole(part, number + 3)

        def correct(i, level=level, size=size):
            level.correct(1 + size * i, size)

        def finish(i, level=level, size=size, target=target, shift=shift):
            target[pl.ds(shift + size * i, size)] = level.finish(1 + size * i, size)

        loop(steps[number], add, steps[number])
        loop(steps[number], correct, steps[number])
        loop(steps[number], finish, steps[number])
        coarse, offset = target, shift

    for pair in range(6):
        parts = []
        for tile in range(3):
            row = 2 * lax.rem(gy - 1 + tile + RING, RING)
            found = answers[2][2 * gz + pair, row // 8]
            found = sub_take(found, lambda s, row=row: lax.rem(row, 8) + s // 4)
            parts.append(lane_take(found, lambda s, l: (s % 2) * 64 + l // 2))
        found = jnp.stack(parts)
        for plane in (2 * pair, 2 * pair + 1):
            two.val[plane] = two.smo[plane] + found
    for at in (1, 6):
        two.correct(at, 5)
    for at in (2, 6):
        answers[1][pl.ds(at, 4)] = two.finish(at, 4)

    def add_one(i):
        for half in (0, 1):
            plane = 1 + 2 * i + half
            parts = []
            for tile in range(8):
                at = tile + 2
                found = sub_take(answers[1][(plane + 4) // 2, at // 4], lambda s, at=at: (at % 4) * 2 + (s // 2) % 2)
                parts.append(lane_take(found, lambda s, l: 64 * (s % 2) + l // 2))
            one.val[plane] = one.smo[plane] + jnp.stack(parts)

    loop(7, add_one, 7)

    def correct_one(i):
        one.correct(2 + 2 * i, 2)

    loop(6, correct_one, 6)

    def finish_one(i):
        answers[0][pl.ds(3 + 2 * i, 2)] = one.finish(3 + 2 * i, 2)

    loop(5, finish_one, 5)

    def add_zero(i):
        parts = []
        for pair in range(10):
            at = pair + 3
            found = sub_take(
                answers[0][i + 3, at // 2],
                lambda s, at=at: (at % 2) * 4 + (s // 4) * 2 + (s % 4) // 2,
            )
            found = lane_take(found, lambda s, l: 64 * (s % 2) + l // 2)
            parts += [found, found]
        added = jnp.stack(parts)
        for plane in (0, 1):
            zero.val[2 * i + plane] = zero.smo[2 * i + plane] + added

    loop(10, add_zero, 2)

    def correct_zero(i):
        for low in (1, 10):
            zero.correct(i + 1, low, 9)

    loop(18, correct_zero, 3)

    def finish_zero(i):
        for low in (2, 10):
            staged[i, pl.ds(low - 2, 8)] = zero.finish(i + 2, low, 8)

    loop(16, finish_zero, 4)

    stores = []
    for group, dst in enumerate((out_a, out_b)):
        for part in range(4):
            copy = pltpu.make_async_copy(
                staged.at[:, :, 4 * group + part], dst.at[:, :, pl.ds(128 * part, 128)], out_sem.at[4 * group + part]
            )
            copy.start()
            stores.append(copy)
    for copy in sent:
        copy.wait_send()
    for slot, ref in ((0, whole[0].mob), (1, whole[0].src)):
        settle(ref, far_send.at[slot, 0], 2 * (RING - 1))
        drain(ref, far_send.at[slot, 1])
    for copy in stores:
        copy.wait()


def scratch_shapes():
    shapes = []

    def arrays(planes, tiles, count=11):
        for _ in range(count):
            shapes.append(pltpu.VMEM((planes, tiles, 8, 128), F32))

    arrays(22, 22, 1)
    arrays(20, 20, 10)
    arrays(16, 8)
    arrays(12, 3)
    for planes, tiles in ((34, 4), (18, 2), (10, 1), (6, 1)):
        arrays(planes, tiles)
    arrays(16, 8, 1)
    arrays(12, 3, 1)
    arrays(36, 4, 1)
    arrays(16, 2, 1)
    arrays(8, 1, 1)
    shapes.append(pltpu.VMEM((22, 22, 8, 128), jnp.int32))
    arrays(16, 16, 1)
    shapes.append(pltpu.VMEM((2, 8, 128), F32))
    shapes.append(pltpu.VMEM((2, 8, 128), F32))
    dma = pltpu.SemaphoreType.DMA
    shapes += [dma((12,)), dma((8,)), dma((7, 8)), dma((7, 8)), dma((2, 3)), dma((2, 2)), pltpu.SemaphoreType.REGULAR((3,))]
    return shapes


def per_device(right_side, cotangent, phase):
    shape = jax.ShapeDtypeStruct(right_side.shape, F32)
    return pl.pallas_call(
        kernel,
        out_shape=(shape, shape),
        in_specs=[pl.BlockSpec(memory_space=pl.ANY)] * 3,
        out_specs=(pl.BlockSpec(memory_space=pl.ANY),) * 2,
        scratch_shapes=scratch_shapes(),
        compiler_params=pltpu.CompilerParams(
            collective_id=0, has_side_effects=True, vmem_limit_bytes=62 * 2**20
        ),
    )(right_side, cotangent, phase)


def solution(mesh):
    spec = P("gz", "gy", None)
    return jax.shard_map(
        per_device, mesh=mesh, in_specs=(spec,) * 3, out_specs=(spec,) * 2, check_vma=False
    )
```

```python
import functools

import jax
import jax.numpy as jnp
from jax import lax
from jax.experimental import pallas as pl
from jax.experimental.pallas import tpu as pltpu
from jax.sharding import PartitionSpec as P

MESH = pl.DeviceIdType.MESH
RING = 16
MID = 1.125
HALF = 0.875
RATIO = MID / HALF
FIRST = 1.0 / RATIO
SECOND = 1.0 / (2.0 * RATIO - FIRST)
C1 = SECOND * FIRST
C2 = 2.0 * SECOND / HALF
LIGHT = 1.0
HEAVY = 1.0 / 8.0
AROUND = ((1, 1), (1, -1), (-1, 1), (-1, -1), (1, 0), (-1, 0), (0, 1), (0, -1))
FAR_Z = (8, 7, 9, 6, 10, 5, 11, 4, 12, 3, 13, 2, 14, 1, 15)
FAR_Y = (10, 6, 9, 11, 14, 7, 5, 13, 2, 8, 15, 1, 3, 12, 4)
F32 = jnp.float32


def flat(values):
    return values.reshape((-1,) + values.shape[-2:])


def sub_iota(shape):
    return lax.broadcasted_iota(jnp.int32, shape, len(shape) - 2)


def lane_iota(shape):
    return lax.broadcasted_iota(jnp.int32, shape, len(shape) - 1)


def sub_take(values, index_of):
    rows = flat(values)
    if rows.shape[0] == 1:
        rows = rows[0]
    index = index_of(sub_iota(rows.shape))
    return jnp.take_along_axis(rows, index, axis=rows.ndim - 2).reshape(values.shape)


def lane_take(values, index_of):
    rows = flat(values)
    if rows.shape[0] == 1:
        rows = rows[0]
    index = index_of(sub_iota(rows.shape), lane_iota(rows.shape))
    return jnp.take_along_axis(rows, index, axis=rows.ndim - 1).reshape(values.shape)


def sub_roll(values, shift):
    rows = flat(values)
    return pltpu.roll(rows, shift % 8, 1).reshape(values.shape)


def lane_roll(values, shift):
    rows = flat(values)
    return pltpu.roll(rows, shift % 128, 2).reshape(values.shape)


class Level:
    def __init__(self, depth, refs):
        self.depth = depth
        self.scale = 0.5 * 0.25**depth
        self.mob, self.src, self.az, self.ay, self.ax, self.bx, self.inv, self.val, self.smo, self.err, self.rem = refs

    def field_one(self, shape):
        if self.depth == 0:
            return sub_iota(shape) >= 4
        if self.depth == 1:
            return (sub_iota(shape) // 2) % 2 == 1
        if self.depth == 2:
            return sub_iota(shape) % 2 == 1
        return lane_iota(shape) >= 64

    def x_side(self, values, step):
        if self.depth <= 2:
            rolled = lane_roll(values, -step)
            if self.depth == 2:
                return rolled
            if self.depth == 0:
                other = sub_take(rolled, lambda s: (s // 4) * 4 + (s + step + 4) % 4)
            else:
                other = sub_take(rolled, lambda s: s + 1 - 2 * (s % 2))
            edge = 127 if step == 1 else 0
            return jnp.where(lane_iota(values.shape) == edge, other, rolled)
        wide = 2 ** (self.depth - 3)
        return lane_take(values, lambda s, l: (l // 64) * 64 + (l + step * wide + 64) % 64)

    def y_side(self, values, step):
        rows = {1: 4, 2: 2}.get(self.depth, 1)
        count = values.shape[1]
        if count == 1:
            other = values
        elif step == 1:
            other = jnp.concatenate([values[:, 1:], values[:, :1]], axis=1)
        else:
            other = jnp.concatenate([values[:, -1:], values[:, :-1]], axis=1)
        place = sub_iota(values.shape)
        edge = place < rows if step == 1 else place >= 8 - rows
        return sub_roll(jnp.where(edge, other, values), -step * rows)

    def coefficients(self, at, count, mask=None):
        here = self.mob[pl.ds(at, count)]
        up = self.scale * (here + self.mob[pl.ds(at + 1, count)])
        down = self.scale * (here + self.mob[pl.ds(at - 1, count)])
        right = self.scale * (here + self.y_side(here, 1))
        ahead = self.scale * (here + self.x_side(here, 1))
        behind = self.scale * (here + self.x_side(here, -1))
        diagonal = up + down + right + self.y_side(right, -1) + ahead + behind
        self.az[pl.ds(at, count)] = up
        self.ay[pl.ds(at, count)] = right
        self.ax[pl.ds(at, count)] = ahead
        self.bx[pl.ds(at, count)] = behind
        return self.masked_inverse(diagonal, mask)

    def masked_inverse(self, diagonal, mask):
        if mask is None:
            return 1.0 / diagonal
        return mask / (diagonal + (1.0 - mask))

    def operate(self, ref, at, count):
        here = ref[pl.ds(at, count)]
        total = self.az[pl.ds(at, count)] * (here - ref[pl.ds(at + 1, count)])
        total = total + self.az[pl.ds(at - 1, count)] * (here - ref[pl.ds(at - 1, count)])
        flux = self.ay[pl.ds(at, count)] * (here - self.y_side(here, 1))
        total = total + (flux - self.y_side(flux, -1))
        total = total + self.ax[pl.ds(at, count)] * (here - self.x_side(here, 1))
        return here, total + self.bx[pl.ds(at, count)] * (here - self.x_side(here, -1))

    def start(self, at, count):
        self.val[pl.ds(at, count)] = self.src[pl.ds(at, count)] * self.inv[pl.ds(at, count)] * (1.0 / MID)

    def smooth(self, at, count):
        here, applied = self.operate(self.val, at, count)
        rest = self.src[pl.ds(at, count)] - applied
        second = here + C1 * here + C2 * (self.inv[pl.ds(at, count)] * rest)
        self.smo[pl.ds(at, count)] = jnp.where(self.field_one(here.shape), here, second)

    def remainder(self, at, count):
        _, applied = self.operate(self.smo, at, count)
        return self.src[pl.ds(at, count)] - applied

    def correct(self, at, count):
        _, applied = self.operate(self.val, at, count)
        rest = self.src[pl.ds(at, count)] - applied
        self.rem[pl.ds(at, count)] = rest
        self.err[pl.ds(at, count)] = rest * self.inv[pl.ds(at, count)] * (1.0 / MID)

    def finish(self, at, count):
        here, applied = self.operate(self.err, at, count)
        rest = self.rem[pl.ds(at, count)] - applied
        second = C1 * here + C2 * (self.inv[pl.ds(at, count)] * rest)
        base = self.val[pl.ds(at, count)] + here
        return jnp.where(self.field_one(here.shape), base + second, base)


class Finest(Level):
    def coefficients(self, plane, low, count, mask):
        here = self.mob[plane + 1, pl.ds(low, count + 2)]
        mid = here[1:-1]
        up = self.scale * (mid + self.mob[plane + 2, pl.ds(low + 1, count)])
        down = self.scale * (mid + self.mob[plane, pl.ds(low + 1, count)])
        right = self.scale * (here[:-1] + here[1:])
        ahead = self.scale * (mid + self.x_side(mid, 1))
        behind = self.scale * (mid + self.x_side(mid, -1))
        diagonal = up + down + right[1:] + right[:-1] + ahead + behind
        self.az[plane, pl.ds(low, count)] = up
        self.ay[plane, pl.ds(low, count)] = right[1:]
        self.ax[plane, pl.ds(low, count)] = ahead
        self.bx[plane, pl.ds(low, count)] = behind
        inverse = self.masked_inverse(diagonal, mask)
        self.inv[plane, pl.ds(low, count)] = inverse
        self.val[plane, pl.ds(low, count)] = self.src[plane, pl.ds(low, count)] * inverse * (1.0 / MID)

    def operate(self, ref, plane, low, count):
        wide = ref[plane, pl.ds(low - 1, count + 2)]
        here = wide[1:-1]
        part = pl.ds(low, count)
        total = self.az[plane, part] * (here - ref[plane + 1, part])
        total = total + self.az[plane - 1, part] * (here - ref[plane - 1, part])
        flux = self.ay[plane, pl.ds(low - 1, count + 1)] * (wide[:-1] - wide[1:])
        total = total + (flux[1:] - flux[:-1])
        total = total + self.ax[plane, part] * (here - self.x_side(here, 1))
        return here, total + self.bx[plane, part] * (here - self.x_side(here, -1))

    def smooth(self, plane, low, count):
        part = pl.ds(low, count)
        here, applied = self.operate(self.val, plane, low, count)
        rest = self.src[plane, part] - applied
        second = here + C1 * here + C2 * (self.inv[plane, part] * rest)
        self.smo[plane, part] = jnp.where(self.field_one(here.shape), here, second)

    def remainder(self, plane, low, count):
        _, applied = self.operate(self.smo, plane, low, count)
        return self.src[plane, pl.ds(low, count)] - applied

    def correct(self, plane, low, count):
        part = pl.ds(low, count)
        _, applied = self.operate(self.val, plane, low, count)
        rest = self.src[plane, part] - applied
        self.rem[plane, part] = rest
        self.err[plane, part] = rest * self.inv[plane, part] * (1.0 / MID)

    def finish(self, plane, low, count):
        part = pl.ds(low, count)
        here, applied = self.operate(self.err, plane, low, count)
        rest = self.rem[plane, part] - applied
        second = C1 * here + C2 * (self.inv[plane, part] * rest)
        base = self.val[plane, part] + here
        return jnp.where(self.field_one(here.shape), base + second, base)


def halves(values):
    return lane_take(values, lambda s, l: (2 * l) % 128) + lane_take(values, lambda s, l: (2 * l + 1) % 128)


def restrict_0(planes):
    count = planes.shape[0] // 4
    four = planes.reshape((count, 4) + planes.shape[1:])
    out = []
    for pair in (0, 2):
        got = halves(four[:, pair] + four[:, pair + 1])
        left = sub_take(got, lambda s: ((s // 2) % 2) * 4 + 2 * (s % 2))
        right = sub_take(got, lambda s: ((s // 2) % 2) * 4 + 2 * (s % 2) + 1)
        out.append(jnp.where(lane_iota(got.shape) < 64, left, right))
    return 0.125 * jnp.where(sub_iota(out[0].shape) < 4, out[0], out[1])


def restrict_1(planes):
    got = halves(planes + sub_roll(planes, 4))
    left = sub_take(got, lambda s: (s % 2) * 2)
    right = sub_take(got, lambda s: (s % 2) * 2 + 1)
    both = jnp.where(lane_iota(got.shape) < 64, left, right)
    row = sub_iota(both[:, 0].shape) // 2
    out = jnp.where(row == 0, both[:, 0], both[:, 1])
    out = jnp.where(row == 2, both[:, 2], out)
    return 0.125 * jnp.where(row == 3, both[:, 3], out)


def restrict_2(planes):
    got = halves(planes + sub_roll(planes, -2))
    left = sub_take(got, lambda s: (4 * s) % 8)
    right = sub_take(got, lambda s: (4 * s + 1) % 8)
    return 0.125 * jnp.where(lane_iota(got.shape) < 64, left, right)


def restrict_whole(planes, depth):
    wide = 2 ** (depth - 3)
    got = planes + lane_take(planes, lambda s, l: l + wide - 2 * wide * ((l // wide) % 2))
    got = sub_take(got + sub_roll(got, -1), lambda s: (2 * s) % 8)
    count = got.shape[1]
    if count == 1:
        return 0.125 * got
    pairs = got.reshape((got.shape[0], count // 2, 2, 8, 128))
    low = sub_iota(pairs[:, :, 0].shape) < 4
    return 0.125 * jnp.where(low, pairs[:, :, 0], pairs[:, :, 1])


def pair_sum(planes):
    pairs = planes.reshape((planes.shape[0] // 2, 2) + planes.shape[1:])
    return pairs[:, 0] + pairs[:, 1]


def twice(planes):
    shape = (planes.shape[0], 2) + planes.shape[1:]
    return jnp.broadcast_to(planes[:, None], shape).reshape((2 * planes.shape[0],) + planes.shape[1:])


def prolong_whole(coarse, depth):
    if depth == 5:
        return twice(sub_take(coarse, lambda s: s // 2))
    low = sub_take(coarse, lambda s: s // 2)
    high = sub_take(coarse, lambda s: 4 + s // 2)
    both = jnp.stack([low, high], axis=2)
    return twice(both.reshape((coarse.shape[0], 2 * coarse.shape[1], 8, 128)))


def loop(count, body, unroll=1):
    def step(i, carry):
        body(i)
        return carry

    lax.fori_loop(0, count, step, 0, unroll=unroll)


def kernel(rhs, cot, phase, out_a, out_b, *scratch):
    scratch = list(scratch)

    def take(count):
        got = scratch[:count]
        del scratch[:count]
        return got

    zero = Finest(0, take(11))
    one, two = Level(1, take(11)), Level(2, take(11))
    whole = [Level(depth, take(11)) for depth in range(3, 7)]
    answers = take(5)
    phases, staged, rows_m, rows_s = take(4)
    in_sem, out_sem, near_send, near_recv, far_send, far_recv, known = take(7)
    gy, gz = lax.axis_index("gy"), lax.axis_index("gz")

    def to_z(step):
        return {"gz": lax.rem(gz + step + RING, RING)}

    def to_y(step):
        return {"gy": lax.rem(gy + step + RING, RING)}

    def to(dy, dz):
        return {"gy": lax.rem(gy + dy + RING, RING), "gz": lax.rem(gz + dz + RING, RING)}

    loads = []
    for group, (src, dst, first) in enumerate(((phase, phases, 0), (rhs, zero.src, 0), (cot, zero.src, 4))):
        edge = 3 if group == 0 else 2
        parts = []
        for part in range(4):
            copy = pltpu.make_async_copy(
                src.at[:, :, pl.ds(128 * part, 128)],
                dst.at[pl.ds(edge, 16), pl.ds(edge, 16), first + part],
                in_sem.at[4 * group + part],
            )
            copy.start()
            parts.append(copy)
        loads.append(parts)

    barrier = pltpu.get_barrier_semaphore()
    for dy, dz in AROUND:
        pl.semaphore_signal(barrier, inc=1, device_id=to(dy, dz), device_id_type=MESH)

    for level in whole:
        count = level.val.shape[0]
        blank = jnp.zeros((1,) + level.val.shape[1:], F32)
        for ref in (level.mob, level.val, level.smo, level.err):
            ref[pl.ds(0, 1)] = blank
            ref[pl.ds(count - 1, 1)] = blank
    for level in whole:
        level.az[pl.ds(0, 1)] = jnp.zeros((1,) + level.val.shape[1:], F32)
    for end in (0, 34):
        answers[2][pl.ds(end, 2)] = jnp.zeros((2, 4, 8, 128), F32)

    def inside(position, extent):
        ok = jnp.logical_and(position >= 0, position < extent)
        return jnp.where(ok, 1.0, 0.0).astype(F32)

    def mobility_of(values, mask):
        found = jnp.where(values == 1, HEAVY, LIGHT).astype(F32) * mask
        return sub_take(found, lambda s: s % 4)

    for copy in loads[0] + loads[1] + loads[2]:
        copy.wait()
    pl.semaphore_wait(barrier, len(AROUND))

    def tell(number):
        away = 2**number
        for device in (to_z(away), to_z(-away), to_y(away), to_y(-away)):
            pl.semaphore_signal(known.at[number], inc=1, device_id=device, device_id_type=MESH)

    tell(0)

    def edges(step, low, size, width):
        if step == 0:
            return low, low, size
        if step == 1:
            return low + size - width, low - width, width
        return low, low + size, width

    def exchange(slot, ref, z_geometry, y_geometry, rows=None):
        copies = []
        for number, (dy, dz) in enumerate(AROUND):
            z_from, z_to, z_count = edges(dz, *z_geometry)
            y_from, y_to, y_count = edges(dy, *y_geometry)
            src = (pl.ds(z_from, z_count), pl.ds(y_from, y_count))
            dst = (pl.ds(z_to, z_count), pl.ds(y_to, y_count))
            if rows is not None:
                src, dst = src + (pl.ds(0, rows),), dst + (pl.ds(0, rows),)
            copy = pltpu.make_async_remote_copy(
                src_ref=ref.at[src],
                dst_ref=ref.at[dst],
                send_sem=near_send.at[slot, number],
                recv_sem=near_recv.at[slot, number],
                device_id=to(dy, dz),
                device_id_type=MESH,
            )
            copy.start()
            copies.append(copy)
        return copies

    def landed(copies):
        for copy in copies:
            copy.wait_recv()

    def place(ref):
        return ref.at[pl.ds(2 * gz + 1, 2), gy // 4, pl.ds(2 * lax.rem(gy, 4), 2)]

    def gather_z(slot, rows, ref):
        own = pltpu.make_async_copy(rows.at[pl.ds(0, 2), pl.ds(0, 2)], place(ref), far_send.at[slot, 2])
        own.start()

        for away in FAR_Z:
            pltpu.make_async_remote_copy(
                src_ref=rows.at[pl.ds(0, 2), pl.ds(0, 2)],
                dst_ref=place(ref),
                send_sem=far_send.at[slot, 0],
                recv_sem=far_recv.at[slot, 0],
                device_id=to_z(away),
                device_id_type=MESH,
            ).start()
        return own

    def settle(ref, semaphore, planes):
        part = ref.at[pl.ds(1, planes), 0, pl.ds(0, 2)]
        pltpu.make_async_copy(part, part, semaphore).wait()

    def gather_y(slot, ref, own):
        own.wait()
        settle(ref, far_recv.at[slot, 0], 2 * (RING - 1))
        part = ref.at[pl.ds(1, 32), gy // 4, pl.ds(2 * lax.rem(gy, 4), 2)]

        for away in FAR_Y:
            pltpu.make_async_remote_copy(
                src_ref=part,
                dst_ref=part,
                send_sem=far_send.at[slot, 1],
                recv_sem=far_recv.at[slot, 1],
                device_id=to_y(away),
                device_id_type=MESH,
            ).start()

    def drain(ref, semaphore):
        part = ref.at[pl.ds(1, 30)]
        pltpu.make_async_copy(part, part, semaphore).wait()

    sent = []
    phase_halo = exchange(0, phases, (3, 16, 3), (3, 16, 3), 4)
    source_halo = exchange(1, zero.src, (2, 16, 2), (2, 16, 2))
    def own_mobility(i):
        total = None
        for plane in (0, 1):
            at = 3 + 2 * i + plane
            found = mobility_of(phases[at, pl.ds(3, 16)], 1.0)
            zero.mob[at, pl.ds(3, 16)] = found
            total = found if total is None else total + found
        one.mob[4 + i, pl.ds(2, 4)] = restrict_0(total)

    loop(8, own_mobility, 2)
    two.mob[pl.ds(4, 4), 1] = restrict_1(pair_sum(one.mob[pl.ds(4, 8), pl.ds(2, 4)]))
    rows_m[...] = restrict_2(pair_sum(two.mob[pl.ds(4, 4), 1]))
    mob_one = exchange(2, one.mob, (4, 8, 4), (2, 4, 2))
    mob_two = exchange(3, two.mob, (4, 4, 4), (1, 1, 1))
    sent += phase_halo + source_halo + mob_one + mob_two

    def z_mask(plane_at, depth, first):
        block = 16 >> depth
        return inside(gz * block + plane_at - first, 256 >> depth)

    pl.semaphore_wait(known.at[0], 4)
    tell(1)

    def inner_coefficients(i):
        zero.coefficients(3 + i, 3, 14, None)

    loop(14, inner_coefficients, 2)
    pl.semaphore_wait(known.at[1], 4)
    tell(2)

    def inner_smooth(i):
        zero.smooth(4 + i, 4, 12)

    loop(12, inner_smooth, 3)
    pl.semaphore_wait(known.at[2], 4)
    own_m = gather_z(0, rows_m, whole[0].mob)
    landed(phase_halo)

    def outer_mobility(i):
        at = jnp.where(i < 3, i, i + 16)
        mask = z_mask(at, 0, 3)
        zero.mob[at, pl.ds(0, 22)] = mobility_of(phases[at, pl.ds(0, 22)], mask)

    loop(6, outer_mobility, 2)

    def side_mobility(i):
        for first in (0, 19):
            zero.mob[3 + i, pl.ds(first, 3)] = mobility_of(phases[3 + i, pl.ds(first, 3)], 1.0)

    loop(16, side_mobility, 4)

    landed(source_halo)

    def outer_coefficients(i):
        at = jnp.where(i < 3, i, i + 14)
        zero.coefficients(at, 0, 20, z_mask(at, 0, 2))

    loop(6, outer_coefficients, 2)

    def side_coefficients(i):
        for low in (0, 17):
            zero.coefficients(3 + i, low, 3, None)

    loop(14, side_coefficients, 7)

    def outer_smooth(i):
        zero.smooth(jnp.where(i < 3, i + 1, i + 13), 1, 18)

    loop(6, outer_smooth, 2)

    def side_smooth(i):
        for low in (1, 16):
            zero.smooth(4 + i, low, 3)

    loop(12, side_smooth, 6)

    for at in (0, 19):
        zero.smo[at] = zero.val[at]

    def ring_zero(i):
        for at in (0, 19):
            zero.smo[i + 1, at] = zero.val[i + 1, at]

    loop(18, ring_zero, 6)

    def remainder_zero(i):
        for half in (0, 1):
            low = 2 + 8 * half
            total = zero.remainder(2 + 2 * i, low, 8) + zero.remainder(3 + 2 * i, low, 8)
            one.src[4 + i, pl.ds(2 + 2 * half, 2)] = restrict_0(total)

    loop(8, remainder_zero, 2)
    source_one = exchange(4, one.src, (4, 8, 3), (2, 4, 2))
    sent += source_one

    gather_y(0, whole[0].mob, own_m)
    landed(mob_one)
    landed(mob_two)

    def fix_mobility(level, planes, depth):
        for at in range(planes):
            level.mob[at] = level.mob[at] * z_mask(at, depth, planes)
            last = level.mob.shape[0] - 1 - at
            level.mob[last] = level.mob[last] * z_mask(last, depth, planes)

    fix_mobility(one, 4, 1)
    fix_mobility(two, 4, 2)

    def masks(at, count, depth, first):
        return jnp.stack([jnp.full((1, 8, 128), z_mask(at + j, depth, first), F32) for j in range(count)])

    def coefficients_one(i):
        at = 1 + 2 * i
        one.inv[pl.ds(at, 2)] = one.coefficients(at, 2, masks(at, 2, 1, 4))

    loop(7, coefficients_one, 7)

    def coefficients_two(i):
        at = 1 + 2 * i
        found = two.coefficients(at, 2, masks(at, 2, 2, 4))
        two.rem[pl.ds(at, 2)] = found

    loop(5, coefficients_two, 5)
    two.az[0] = two.scale * (two.mob[0] + two.mob[1])
    two.inv[pl.ds(4, 4), 1] = two.rem[pl.ds(4, 4), 1]
    inverse_two = exchange(5, two.inv, (4, 4, 4), (1, 1, 1))
    sent += inverse_two

    landed(source_one)

    def start_one(i):
        one.start(1 + 2 * i, 2)

    loop(7, start_one, 7)

    def smooth_one(i):
        one.smooth(2 + 2 * i, 2)

    loop(6, smooth_one, 6)
    for at in (1, 14):
        one.smo[at] = one.val[at]

    def remainder_one(i):
        rest = one.remainder(4 + 2 * i, 2)[:, 2:6]
        two.src[pl.ds(4 + i, 1), 1] = restrict_1(pair_sum(rest))[0:1]

    loop(4, remainder_one, 4)
    source_two = exchange(6, two.src, (4, 4, 4), (1, 1, 1))
    sent += source_two

    landed(inverse_two)
    for at in (0, 1, 2, 3, 8, 9, 10, 11):
        two.inv[at] = two.inv[at] * z_mask(at, 2, 4)
    landed(source_two)
    for at in (0, 4, 8):
        two.start(at, 4)
    two.smooth(2, 4)
    two.smooth(6, 4)
    for at in (0, 1, 10, 11):
        two.smo[at] = two.val[at]
    rows_s[...] = restrict_2(pair_sum(two.remainder(4, 4)[:, 1]))
    own_s = gather_z(1, rows_s, whole[0].src)

    drain(whole[0].mob, far_recv.at[0, 1])

    block = (4, 8, 8, 4)
    steps = (8, 2, 1, 1)
    for number, level in enumerate(whole):
        size = block[number]
        if number > 0:
            finer = whole[number - 1]

            def coarsen(i, finer=finer, level=level, size=size, number=number):
                total = pair_sum(finer.mob[pl.ds(1 + 2 * size * i, 2 * size)])
                level.mob[pl.ds(1 + size * i, size)] = restrict_whole(total, number + 2)

            loop(steps[number], coarsen, steps[number])

        level.az[pl.ds(0, 1)] = level.scale * level.mob[pl.ds(1, 1)]

        def coefficients(i, level=level, size=size):
            at = 1 + size * i
            level.inv[pl.ds(at, size)] = level.coefficients(at, size)

        loop(steps[number], coefficients, steps[number])

    gather_y(1, whole[0].src, own_s)
    drain(whole[0].src, far_recv.at[1, 1])

    for number, level in enumerate(whole[:-1]):
        size = block[number]
        coarser = whole[number + 1]

        def start(i, level=level, size=size):
            level.start(1 + size * i, size)

        def smooth(i, level=level, size=size):
            level.smooth(1 + size * i, size)

        def lower(i, level=level, size=size, coarser=coarser, number=number):
            rest = pair_sum(level.remainder(1 + size * i, size))
            coarser.src[pl.ds(1 + (size // 2) * i, size // 2)] = restrict_whole(rest, number + 3)

        loop(steps[number], start, steps[number])
        loop(steps[number], smooth, steps[number])
        loop(steps[number], lower, steps[number])

    last = whole[-1]
    last.start(1, 4)
    iterate = last.val[pl.ds(1, 4)]
    direction = iterate
    factor = FIRST
    for _ in range(3):
        _, applied = last.operate(last.val, 1, 4)
        following = 1.0 / (2.0 * RATIO - factor)
        rest = last.src[pl.ds(1, 4)] - applied
        direction = (following * factor) * direction + (2.0 * following / HALF) * (last.inv[pl.ds(1, 4)] * rest)
        iterate = iterate + direction
        last.val[pl.ds(1, 4)] = iterate
        factor = following
    coarse, offset = last.val, 1

    for number in (2, 1, 0):
        level = whole[number]
        size = block[number]
        target, shift = ((answers[2], 2), (answers[3], 0), (answers[4], 0))[number]

        def add(i, level=level, size=size, coarse=coarse, offset=offset, number=number):
            part = coarse[pl.ds(offset + (size // 2) * i, size // 2)]
            at = 1 + size * i
            level.val[pl.ds(at, size)] = level.smo[pl.ds(at, size)] + prolong_whole(part, number + 3)

        def correct(i, level=level, size=size):
            level.correct(1 + size * i, size)

        def finish(i, level=level, size=size, target=target, shift=shift):
            target[pl.ds(shift + size * i, size)] = level.finish(1 + size * i, size)

        loop(steps[number], add, steps[number])
        loop(steps[number], correct, steps[number])
        loop(steps[number], finish, steps[number])
        coarse, offset = target, shift

    for pair in range(6):
        parts = []
        for tile in range(3):
            row = 2 * lax.rem(gy - 1 + tile + RING, RING)
            found = answers[2][2 * gz + pair, row // 8]
            found = sub_take(found, lambda s, row=row: lax.rem(row, 8) + s // 4)
            parts.append(lane_take(found, lambda s, l: (s % 2) * 64 + l // 2))
        found = jnp.stack(parts)
        for plane in (2 * pair, 2 * pair + 1):
            two.val[plane] = two.smo[plane] + found
    for at in (1, 6):
        two.correct(at, 5)
    for at in (2, 6):
        answers[1][pl.ds(at, 4)] = two.finish(at, 4)

    def add_one(i):
        for half in (0, 1):
            plane = 1 + 2 * i + half
            parts = []
            for tile in range(8):
                at = tile + 2
                found = sub_take(answers[1][(plane + 4) // 2, at // 4], lambda s, at=at: (at % 4) * 2 + (s // 2) % 2)
                parts.append(lane_take(found, lambda s, l: 64 * (s % 2) + l // 2))
            one.val[plane] = one.smo[plane] + jnp.stack(parts)

    loop(7, add_one, 7)

    def correct_one(i):
        one.correct(2 + 2 * i, 2)

    loop(6, correct_one, 6)

    def finish_one(i):
        answers[0][pl.ds(3 + 2 * i, 2)] = one.finish(3 + 2 * i, 2)

    loop(5, finish_one, 5)

    def add_zero(i):
        parts = []
        for pair in range(10):
            at = pair + 3
            found = sub_take(
                answers[0][i + 3, at // 2],
                lambda s, at=at: (at % 2) * 4 + (s // 4) * 2 + (s % 4) // 2,
            )
            found = lane_take(found, lambda s, l: 64 * (s % 2) + l // 2)
            parts += [found, found]
        added = jnp.stack(parts)
        for plane in (0, 1):
            zero.val[2 * i + plane] = zero.smo[2 * i + plane] + added

    loop(10, add_zero, 2)

    def correct_zero(i):
        for low in (1, 10):
            zero.correct(i + 1, low, 9)

    loop(18, correct_zero, 3)

    stores = []
    for begin, count in ((0, 8), (8, 4), (12, 4)):

        def finish_zero(i, begin=begin):
            for low in (2, 10):
                staged[begin + i, pl.ds(low - 2, 8)] = zero.finish(begin + i + 2, low, 8)

        loop(count, finish_zero, 4)
        planes = pl.ds(begin, count)
        for group, dst in enumerate((out_a, out_b)):
            for part in range(4):
                copy = pltpu.make_async_copy(
                    staged.at[planes, :, 4 * group + part],
                    dst.at[planes, :, pl.ds(128 * part, 128)],
                    out_sem.at[len(stores)],
                )
                copy.start()
                stores.append(copy)
    for copy in sent:
        copy.wait_send()
    for slot, ref in ((0, whole[0].mob), (1, whole[0].src)):
        settle(ref, far_send.at[slot, 0], 2 * (RING - 1))
        drain(ref, far_send.at[slot, 1])
    for copy in stores:
        copy.wait()


def scratch_shapes():
    shapes = []

    def arrays(planes, tiles, count=11):
        for _ in range(count):
            shapes.append(pltpu.VMEM((planes, tiles, 8, 128), F32))

    arrays(22, 22, 1)
    arrays(20, 20, 10)
    arrays(16, 8)
    arrays(12, 3)
    for planes, tiles in ((34, 4), (18, 2), (10, 1), (6, 1)):
        arrays(planes, tiles)
    arrays(16, 8, 1)
    arrays(12, 3, 1)
    arrays(36, 4, 1)
    arrays(16, 2, 1)
    arrays(8, 1, 1)
    shapes.append(pltpu.VMEM((22, 22, 8, 128), jnp.int32))
    arrays(16, 16, 1)
    shapes.append(pltpu.VMEM((2, 8, 128), F32))
    shapes.append(pltpu.VMEM((2, 8, 128), F32))
    dma = pltpu.SemaphoreType.DMA
    shapes += [dma((12,)), dma((24,)), dma((7, 8)), dma((7, 8)), dma((2, 3)), dma((2, 2)), pltpu.SemaphoreType.REGULAR((3,))]
    return shapes


def per_device(right_side, cotangent, phase):
    shape = jax.ShapeDtypeStruct(right_side.shape, F32)
    return pl.pallas_call(
        kernel,
        out_shape=(shape, shape),
        in_specs=[pl.BlockSpec(memory_space=pl.ANY)] * 3,
        out_specs=(pl.BlockSpec(memory_space=pl.ANY),) * 2,
        scratch_shapes=scratch_shapes(),
        compiler_params=pltpu.CompilerParams(
            collective_id=0, has_side_effects=True, vmem_limit_bytes=62 * 2**20
        ),
    )(right_side, cotangent, phase)


def solution(mesh):
    spec = P("gz", "gy", None)
    return jax.shard_map(
        per_device, mesh=mesh, in_specs=(spec,) * 3, out_specs=(spec,) * 2, check_vma=False
    )
```

```python
import functools

import jax
import jax.numpy as jnp
from jax import lax
from jax.experimental import pallas as pl
from jax.experimental.pallas import tpu as pltpu
from jax.sharding import PartitionSpec as P

MESH = pl.DeviceIdType.MESH
RING = 16
MID = 1.125
HALF = 0.875
RATIO = MID / HALF
FIRST = 1.0 / RATIO
SECOND = 1.0 / (2.0 * RATIO - FIRST)
C1 = SECOND * FIRST
C2 = 2.0 * SECOND / HALF
LIGHT = 1.0
HEAVY = 1.0 / 8.0
AROUND = ((1, 0), (-1, 0), (1, 1), (1, -1), (-1, 1), (-1, -1), (0, 1), (0, -1))
FAR_Z = tuple(range(1, 16))
FAR_Y = tuple(range(1, 16))
F32 = jnp.float32


def flat(values):
    return values.reshape((-1,) + values.shape[-2:])


def sub_iota(shape):
    return lax.broadcasted_iota(jnp.int32, shape, len(shape) - 2)


def lane_iota(shape):
    return lax.broadcasted_iota(jnp.int32, shape, len(shape) - 1)


def sub_take(values, index_of):
    rows = flat(values)
    if rows.shape[0] == 1:
        rows = rows[0]
    index = index_of(sub_iota(rows.shape))
    return jnp.take_along_axis(rows, index, axis=rows.ndim - 2).reshape(values.shape)


def lane_take(values, index_of):
    rows = flat(values)
    if rows.shape[0] == 1:
        rows = rows[0]
    index = index_of(sub_iota(rows.shape), lane_iota(rows.shape))
    return jnp.take_along_axis(rows, index, axis=rows.ndim - 1).reshape(values.shape)


def sub_roll(values, shift):
    rows = flat(values)
    return pltpu.roll(rows, shift % 8, 1).reshape(values.shape)


def lane_roll(values, shift):
    rows = flat(values)
    return pltpu.roll(rows, shift % 128, 2).reshape(values.shape)


class Level:
    def __init__(self, depth, refs):
        self.depth = depth
        self.scale = 0.5 * 0.25**depth
        self.mob, self.src, self.az, self.ay, self.ax, self.bx, self.inv, self.val, self.smo, self.err, self.rem = refs

    def field_one(self, shape):
        if self.depth == 0:
            return sub_iota(shape) >= 4
        if self.depth == 1:
            return (sub_iota(shape) // 2) % 2 == 1
        if self.depth == 2:
            return sub_iota(shape) % 2 == 1
        return lane_iota(shape) >= 64

    def x_side(self, values, step):
        if self.depth <= 2:
            rolled = lane_roll(values, -step)
            if self.depth == 2:
                return rolled
            if self.depth == 0:
                other = sub_take(rolled, lambda s: (s // 4) * 4 + (s + step + 4) % 4)
            else:
                other = sub_take(rolled, lambda s: s + 1 - 2 * (s % 2))
            edge = 127 if step == 1 else 0
            return jnp.where(lane_iota(values.shape) == edge, other, rolled)
        wide = 2 ** (self.depth - 3)
        return lane_take(values, lambda s, l: (l // 64) * 64 + (l + step * wide + 64) % 64)

    def y_side(self, values, step):
        rows = {1: 4, 2: 2}.get(self.depth, 1)
        count = values.shape[1]
        if count == 1:
            other = values
        elif step == 1:
            other = jnp.concatenate([values[:, 1:], values[:, :1]], axis=1)
        else:
            other = jnp.concatenate([values[:, -1:], values[:, :-1]], axis=1)
        place = sub_iota(values.shape)
        edge = place < rows if step == 1 else place >= 8 - rows
        return sub_roll(jnp.where(edge, other, values), -step * rows)

    def coefficients(self, at, count, mask=None):
        here = self.mob[pl.ds(at, count)]
        up = self.scale * (here + self.mob[pl.ds(at + 1, count)])
        down = self.scale * (here + self.mob[pl.ds(at - 1, count)])
        right = self.scale * (here + self.y_side(here, 1))
        ahead = self.scale * (here + self.x_side(here, 1))
        behind = self.scale * (here + self.x_side(here, -1))
        diagonal = up + down + right + self.y_side(right, -1) + ahead + behind
        self.az[pl.ds(at, count)] = up
        self.ay[pl.ds(at, count)] = right
        self.ax[pl.ds(at, count)] = ahead
        self.bx[pl.ds(at, count)] = behind
        return self.masked_inverse(diagonal, mask)

    def masked_inverse(self, diagonal, mask):
        if mask is None:
            return 1.0 / diagonal
        return mask / (diagonal + (1.0 - mask))

    def operate(self, ref, at, count):
        here = ref[pl.ds(at, count)]
        total = self.az[pl.ds(at, count)] * (here - ref[pl.ds(at + 1, count)])
        total = total + self.az[pl.ds(at - 1, count)] * (here - ref[pl.ds(at - 1, count)])
        flux = self.ay[pl.ds(at, count)] * (here - self.y_side(here, 1))
        total = total + (flux - self.y_side(flux, -1))
        total = total + self.ax[pl.ds(at, count)] * (here - self.x_side(here, 1))
        return here, total + self.bx[pl.ds(at, count)] * (here - self.x_side(here, -1))

    def start(self, at, count):
        self.val[pl.ds(at, count)] = self.src[pl.ds(at, count)] * self.inv[pl.ds(at, count)] * (1.0 / MID)

    def smooth(self, at, count):
        here, applied = self.operate(self.val, at, count)
        rest = self.src[pl.ds(at, count)] - applied
        second = here + C1 * here + C2 * (self.inv[pl.ds(at, count)] * rest)
        self.smo[pl.ds(at, count)] = jnp.where(self.field_one(here.shape), here, second)

    def remainder(self, at, count):
        _, applied = self.operate(self.smo, at, count)
        return self.src[pl.ds(at, count)] - applied

    def correct(self, at, count):
        _, applied = self.operate(self.val, at, count)
        rest = self.src[pl.ds(at, count)] - applied
        self.rem[pl.ds(at, count)] = rest
        self.err[pl.ds(at, count)] = rest * self.inv[pl.ds(at, count)] * (1.0 / MID)

    def finish(self, at, count):
        here, applied = self.operate(self.err, at, count)
        rest = self.rem[pl.ds(at, count)] - applied
        second = C1 * here + C2 * (self.inv[pl.ds(at, count)] * rest)
        base = self.val[pl.ds(at, count)] + here
        return jnp.where(self.field_one(here.shape), base + second, base)


class Finest(Level):
    def coefficients(self, plane, low, count, mask):
        here = self.mob[plane + 1, pl.ds(low, count + 2)]
        mid = here[1:-1]
        up = self.scale * (mid + self.mob[plane + 2, pl.ds(low + 1, count)])
        down = self.scale * (mid + self.mob[plane, pl.ds(low + 1, count)])
        right = self.scale * (here[:-1] + here[1:])
        ahead = self.scale * (mid + self.x_side(mid, 1))
        behind = self.scale * (mid + self.x_side(mid, -1))
        diagonal = up + down + right[1:] + right[:-1] + ahead + behind
        self.az[plane, pl.ds(low, count)] = up
        self.ay[plane, pl.ds(low, count)] = right[1:]
        self.ax[plane, pl.ds(low, count)] = ahead
        self.bx[plane, pl.ds(low, count)] = behind
        inverse = self.masked_inverse(diagonal, mask)
        self.inv[plane, pl.ds(low, count)] = inverse
        self.val[plane, pl.ds(low, count)] = self.src[plane, pl.ds(low, count)] * inverse * (1.0 / MID)

    def operate(self, ref, plane, low, count):
        wide = ref[plane, pl.ds(low - 1, count + 2)]
        here = wide[1:-1]
        part = pl.ds(low, count)
        total = self.az[plane, part] * (here - ref[plane + 1, part])
        total = total + self.az[plane - 1, part] * (here - ref[plane - 1, part])
        flux = self.ay[plane, pl.ds(low - 1, count + 1)] * (wide[:-1] - wide[1:])
        total = total + (flux[1:] - flux[:-1])
        total = total + self.ax[plane, part] * (here - self.x_side(here, 1))
        return here, total + self.bx[plane, part] * (here - self.x_side(here, -1))

    def smooth(self, plane, low, count):
        part = pl.ds(low, count)
        here, applied = self.operate(self.val, plane, low, count)
        rest = self.src[plane, part] - applied
        second = here + C1 * here + C2 * (self.inv[plane, part] * rest)
        self.smo[plane, part] = jnp.where(self.field_one(here.shape), here, second)

    def remainder(self, plane, low, count):
        _, applied = self.operate(self.smo, plane, low, count)
        return self.src[plane, pl.ds(low, count)] - applied

    def correct(self, plane, low, count):
        part = pl.ds(low, count)
        _, applied = self.operate(self.val, plane, low, count)
        rest = self.src[plane, part] - applied
        self.rem[plane, part] = rest
        self.err[plane, part] = rest * self.inv[plane, part] * (1.0 / MID)

    def finish(self, plane, low, count):
        part = pl.ds(low, count)
        here, applied = self.operate(self.err, plane, low, count)
        rest = self.rem[plane, part] - applied
        second = C1 * here + C2 * (self.inv[plane, part] * rest)
        base = self.val[plane, part] + here
        return jnp.where(self.field_one(here.shape), base + second, base)


def halves(values):
    return lane_take(values, lambda s, l: (2 * l) % 128) + lane_take(values, lambda s, l: (2 * l + 1) % 128)


def restrict_0(planes):
    count = planes.shape[0] // 4
    four = planes.reshape((count, 4) + planes.shape[1:])
    out = []
    for pair in (0, 2):
        got = halves(four[:, pair] + four[:, pair + 1])
        left = sub_take(got, lambda s: ((s // 2) % 2) * 4 + 2 * (s % 2))
        right = sub_take(got, lambda s: ((s // 2) % 2) * 4 + 2 * (s % 2) + 1)
        out.append(jnp.where(lane_iota(got.shape) < 64, left, right))
    return 0.125 * jnp.where(sub_iota(out[0].shape) < 4, out[0], out[1])


def restrict_1(planes):
    got = halves(planes + sub_roll(planes, 4))
    left = sub_take(got, lambda s: (s % 2) * 2)
    right = sub_take(got, lambda s: (s % 2) * 2 + 1)
    both = jnp.where(lane_iota(got.shape) < 64, left, right)
    row = sub_iota(both[:, 0].shape) // 2
    out = jnp.where(row == 0, both[:, 0], both[:, 1])
    out = jnp.where(row == 2, both[:, 2], out)
    return 0.125 * jnp.where(row == 3, both[:, 3], out)


def restrict_2(planes):
    got = halves(planes + sub_roll(planes, -2))
    left = sub_take(got, lambda s: (4 * s) % 8)
    right = sub_take(got, lambda s: (4 * s + 1) % 8)
    return 0.125 * jnp.where(lane_iota(got.shape) < 64, left, right)


def restrict_whole(planes, depth):
    wide = 2 ** (depth - 3)
    got = planes + lane_take(planes, lambda s, l: l + wide - 2 * wide * ((l // wide) % 2))
    got = sub_take(got + sub_roll(got, -1), lambda s: (2 * s) % 8)
    count = got.shape[1]
    if count == 1:
        return 0.125 * got
    pairs = got.reshape((got.shape[0], count // 2, 2, 8, 128))
    low = sub_iota(pairs[:, :, 0].shape) < 4
    return 0.125 * jnp.where(low, pairs[:, :, 0], pairs[:, :, 1])


def pair_sum(planes):
    pairs = planes.reshape((planes.shape[0] // 2, 2) + planes.shape[1:])
    return pairs[:, 0] + pairs[:, 1]


def twice(planes):
    shape = (planes.shape[0], 2) + planes.shape[1:]
    return jnp.broadcast_to(planes[:, None], shape).reshape((2 * planes.shape[0],) + planes.shape[1:])


def prolong_whole(coarse, depth):
    if depth == 5:
        return twice(sub_take(coarse, lambda s: s // 2))
    low = sub_take(coarse, lambda s: s // 2)
    high = sub_take(coarse, lambda s: 4 + s // 2)
    both = jnp.stack([low, high], axis=2)
    return twice(both.reshape((coarse.shape[0], 2 * coarse.shape[1], 8, 128)))


def loop(count, body, unroll=1):
    def step(i, carry):
        body(i)
        return carry

    lax.fori_loop(0, count, step, 0, unroll=unroll)


def kernel(rhs, cot, phase, both, *scratch):
    scratch = list(scratch)

    def take(count):
        got = scratch[:count]
        del scratch[:count]
        return got

    zero = Finest(0, take(11))
    one, two = Level(1, take(11)), Level(2, take(11))
    whole = [Level(depth, take(11)) for depth in range(3, 7)]
    answers = take(5)
    phases, staged, rows_m, rows_s = take(4)
    in_sem, out_sem, near_send, near_recv, far_send, far_recv, known = take(7)
    gy, gz = lax.axis_index("gy"), lax.axis_index("gz")

    def to_z(step):
        return {"gz": lax.rem(gz + step + RING, RING)}

    def to_y(step):
        return {"gy": lax.rem(gy + step + RING, RING)}

    def to(dy, dz):
        return {"gy": lax.rem(gy + dy + RING, RING), "gz": lax.rem(gz + dz + RING, RING)}

    barrier = pltpu.get_barrier_semaphore()
    for dy, dz in AROUND:
        pl.semaphore_signal(barrier, inc=1, device_id=to(dy, dz), device_id_type=MESH)

    loads = []
    for group, (src, dst, first) in enumerate(((phase, phases, 0), (rhs, zero.src, 0), (cot, zero.src, 4))):
        edge = 3 if group == 0 else 2
        parts = []
        for part in range(4):
            copy = pltpu.make_async_copy(
                src.at[:, :, pl.ds(128 * part, 128)],
                dst.at[pl.ds(edge, 16), pl.ds(edge, 16), first + part],
                in_sem.at[4 * group + part],
            )
            copy.start()
            parts.append(copy)
        loads.append(parts)


    for level in whole:
        count = level.val.shape[0]
        blank = jnp.zeros((1,) + level.val.shape[1:], F32)
        for ref in (level.mob, level.val, level.smo, level.err):
            ref[pl.ds(0, 1)] = blank
            ref[pl.ds(count - 1, 1)] = blank
    for level in whole:
        level.az[pl.ds(0, 1)] = jnp.zeros((1,) + level.val.shape[1:], F32)
    for end in (0, 34):
        answers[2][pl.ds(end, 2)] = jnp.zeros((2, 4, 8, 128), F32)

    def inside(position, extent):
        ok = jnp.logical_and(position >= 0, position < extent)
        return jnp.where(ok, 1.0, 0.0).astype(F32)

    def mobility_of(values, mask):
        found = jnp.where(values == 1, HEAVY, LIGHT).astype(F32) * mask
        return sub_take(found, lambda s: s % 4)

    for copy in loads[0]:
        copy.wait()
    pl.semaphore_wait(barrier, len(AROUND))

    def tell(number):
        away = 2**number
        for device in (to_z(away), to_z(-away), to_y(away), to_y(-away)):
            pl.semaphore_signal(known.at[number], inc=1, device_id=device, device_id_type=MESH)

    tell(0)

    def edges(step, low, size, width):
        if step == 0:
            return low, low, size
        if step == 1:
            return low + size - width, low - width, width
        return low, low + size, width

    def exchange(slot, ref, z_geometry, y_geometry, rows=None, corner=None):
        copies = []
        for number, (dy, dz) in enumerate(AROUND):
            both = corner is not None and dy != 0 and dz != 0
            z_from, z_to, z_count = edges(dz, *(z_geometry[:2] + (corner,) if both else z_geometry))
            y_from, y_to, y_count = edges(dy, *(y_geometry[:2] + (corner,) if both else y_geometry))
            src = (pl.ds(z_from, z_count), pl.ds(y_from, y_count))
            dst = (pl.ds(z_to, z_count), pl.ds(y_to, y_count))
            if rows is not None:
                src, dst = src + (pl.ds(0, rows),), dst + (pl.ds(0, rows),)
            copy = pltpu.make_async_remote_copy(
                src_ref=ref.at[src],
                dst_ref=ref.at[dst],
                send_sem=near_send.at[slot, number],
                recv_sem=near_recv.at[slot, number],
                device_id=to(dy, dz),
                device_id_type=MESH,
            )
            copy.start()
            copies.append(copy)
        return copies

    def landed(copies):
        for copy in copies:
            copy.wait_recv()

    def place(ref):
        return ref.at[pl.ds(2 * gz + 1, 2), gy // 4, pl.ds(2 * lax.rem(gy, 4), 2)]

    def gather_z(slot, rows, ref):
        own = pltpu.make_async_copy(rows.at[pl.ds(0, 2), pl.ds(0, 2)], place(ref), far_send.at[slot, 2])
        own.start()

        for away in FAR_Z:
            pltpu.make_async_remote_copy(
                src_ref=rows.at[pl.ds(0, 2), pl.ds(0, 2)],
                dst_ref=place(ref),
                send_sem=far_send.at[slot, 0],
                recv_sem=far_recv.at[slot, 0],
                device_id=to_z(away),
                device_id_type=MESH,
            ).start()
        return own

    def settle(ref, semaphore, planes):
        part = ref.at[pl.ds(1, planes), 0, pl.ds(0, 2)]
        pltpu.make_async_copy(part, part, semaphore).wait()

    def gather_y(slot, ref, own):
        own.wait()
        settle(ref, far_recv.at[slot, 0], 2 * (RING - 1))
        part = ref.at[pl.ds(1, 32), gy // 4, pl.ds(2 * lax.rem(gy, 4), 2)]

        for away in FAR_Y:
            pltpu.make_async_remote_copy(
                src_ref=part,
                dst_ref=part,
                send_sem=far_send.at[slot, 1],
                recv_sem=far_recv.at[slot, 1],
                device_id=to_y(away),
                device_id_type=MESH,
            ).start()

    def drain(ref, semaphore):
        part = ref.at[pl.ds(1, 30)]
        pltpu.make_async_copy(part, part, semaphore).wait()

    sent = []
    phase_halo = exchange(0, phases, (3, 16, 3), (3, 16, 3), 4, 2)
    for copy in loads[1] + loads[2]:
        copy.wait()
    source_halo = exchange(1, zero.src, (2, 16, 2), (2, 16, 2), None, 1)
    def own_mobility(i):
        total = None
        for plane in (0, 1):
            at = 3 + 2 * i + plane
            found = mobility_of(phases[at, pl.ds(3, 16)], 1.0)
            zero.mob[at, pl.ds(3, 16)] = found
            total = found if total is None else total + found
        one.mob[4 + i, pl.ds(2, 4)] = restrict_0(total)

    loop(8, own_mobility, 2)
    two.mob[pl.ds(4, 4), 1] = restrict_1(pair_sum(one.mob[pl.ds(4, 8), pl.ds(2, 4)]))
    rows_m[...] = restrict_2(pair_sum(two.mob[pl.ds(4, 4), 1]))
    mob_one = exchange(2, one.mob, (4, 8, 4), (2, 4, 2))
    mob_two = exchange(3, two.mob, (4, 4, 4), (1, 1, 1))
    sent += phase_halo + source_halo + mob_one + mob_two

    def z_mask(plane_at, depth, first):
        block = 16 >> depth
        return inside(gz * block + plane_at - first, 256 >> depth)

    pl.semaphore_wait(known.at[0], 4)
    tell(1)

    def inner_coefficients(i):
        zero.coefficients(3 + i, 3, 14, None)

    loop(14, inner_coefficients, 2)
    pl.semaphore_wait(known.at[1], 4)
    tell(2)

    def inner_smooth(i):
        zero.smooth(4 + i, 4, 12)

    loop(12, inner_smooth, 3)
    pl.semaphore_wait(known.at[2], 4)
    own_m = gather_z(0, rows_m, whole[0].mob)
    landed(phase_halo)

    def outer_mobility(i):
        at = jnp.where(i < 3, i, i + 16)
        mask = z_mask(at, 0, 3)
        zero.mob[at, pl.ds(0, 22)] = mobility_of(phases[at, pl.ds(0, 22)], mask)

    loop(6, outer_mobility, 2)

    def side_mobility(i):
        for first in (0, 19):
            zero.mob[3 + i, pl.ds(first, 3)] = mobility_of(phases[3 + i, pl.ds(first, 3)], 1.0)

    loop(16, side_mobility, 4)

    landed(source_halo)

    def outer_coefficients(i):
        at = jnp.where(i < 3, i, i + 14)
        zero.coefficients(at, 0, 20, z_mask(at, 0, 2))

    loop(6, outer_coefficients, 2)

    def side_coefficients(i):
        for low in (0, 17):
            zero.coefficients(3 + i, low, 3, None)

    loop(14, side_coefficients, 7)

    def outer_smooth(i):
        zero.smooth(jnp.where(i < 3, i + 1, i + 13), 1, 18)

    loop(6, outer_smooth, 2)

    def side_smooth(i):
        for low in (1, 16):
            zero.smooth(4 + i, low, 3)

    loop(12, side_smooth, 6)

    for at in (0, 19):
        zero.smo[at] = zero.val[at]

    def ring_zero(i):
        for at in (0, 19):
            zero.smo[i + 1, at] = zero.val[i + 1, at]

    loop(18, ring_zero, 6)

    def remainder_zero(i):
        for half in (0, 1):
            low = 2 + 8 * half
            total = zero.remainder(2 + 2 * i, low, 8) + zero.remainder(3 + 2 * i, low, 8)
            one.src[4 + i, pl.ds(2 + 2 * half, 2)] = restrict_0(total)

    loop(8, remainder_zero, 4)
    source_one = exchange(4, one.src, (4, 8, 3), (2, 4, 2))
    sent += source_one

    landed(mob_one)
    landed(mob_two)

    def fix_mobility(level, planes, depth):
        for at in range(planes):
            level.mob[at] = level.mob[at] * z_mask(at, depth, planes)
            last = level.mob.shape[0] - 1 - at
            level.mob[last] = level.mob[last] * z_mask(last, depth, planes)

    fix_mobility(one, 4, 1)
    fix_mobility(two, 4, 2)

    def masks(at, count, depth, first):
        return jnp.stack([jnp.full((1, 8, 128), z_mask(at + j, depth, first), F32) for j in range(count)])

    def coefficients_one(i):
        at = 1 + 2 * i
        one.inv[pl.ds(at, 2)] = one.coefficients(at, 2, masks(at, 2, 1, 4))

    loop(7, coefficients_one, 7)

    def coefficients_two(i):
        at = 1 + 2 * i
        found = two.coefficients(at, 2, masks(at, 2, 2, 4))
        two.rem[pl.ds(at, 2)] = found

    loop(5, coefficients_two, 5)
    two.az[0] = two.scale * (two.mob[0] + two.mob[1])
    two.inv[pl.ds(4, 4), 1] = two.rem[pl.ds(4, 4), 1]
    inverse_two = exchange(5, two.inv, (4, 4, 4), (1, 1, 1))
    sent += inverse_two

    landed(source_one)

    def start_one(i):
        one.start(1 + 2 * i, 2)

    loop(7, start_one, 7)

    def smooth_one(i):
        one.smooth(2 + 2 * i, 2)

    loop(6, smooth_one, 6)
    for at in (1, 14):
        one.smo[at] = one.val[at]

    def remainder_one(i):
        rest = one.remainder(4 + 2 * i, 2)[:, 2:6]
        two.src[pl.ds(4 + i, 1), 1] = restrict_1(pair_sum(rest))[0:1]

    loop(4, remainder_one, 4)
    source_two = exchange(6, two.src, (4, 4, 4), (1, 1, 1))
    sent += source_two
    gather_y(0, whole[0].mob, own_m)

    landed(inverse_two)
    for at in (0, 1, 2, 3, 8, 9, 10, 11):
        two.inv[at] = two.inv[at] * z_mask(at, 2, 4)
    landed(source_two)
    for at in (0, 4, 8):
        two.start(at, 4)
    two.smooth(2, 4)
    two.smooth(6, 4)
    for at in (0, 1, 10, 11):
        two.smo[at] = two.val[at]
    rows_s[...] = restrict_2(pair_sum(two.remainder(4, 4)[:, 1]))
    own_s = gather_z(1, rows_s, whole[0].src)

    gather_y(1, whole[0].src, own_s)

    drain(whole[0].mob, far_recv.at[0, 1])

    block = (4, 8, 8, 4)
    steps = (8, 2, 1, 1)
    for number, level in enumerate(whole):
        size = block[number]
        if number > 0:
            finer = whole[number - 1]

            def coarsen(i, finer=finer, level=level, size=size, number=number):
                total = pair_sum(finer.mob[pl.ds(1 + 2 * size * i, 2 * size)])
                level.mob[pl.ds(1 + size * i, size)] = restrict_whole(total, number + 2)

            loop(steps[number], coarsen, steps[number])

        level.az[pl.ds(0, 1)] = level.scale * level.mob[pl.ds(1, 1)]

        def coefficients(i, level=level, size=size):
            at = 1 + size * i
            level.inv[pl.ds(at, size)] = level.coefficients(at, size)

        loop(steps[number], coefficients, steps[number])

    drain(whole[0].src, far_recv.at[1, 1])

    for number, level in enumerate(whole[:-1]):
        size = block[number]
        coarser = whole[number + 1]

        def start(i, level=level, size=size):
            level.start(1 + size * i, size)

        def smooth(i, level=level, size=size):
            level.smooth(1 + size * i, size)

        def lower(i, level=level, size=size, coarser=coarser, number=number):
            rest = pair_sum(level.remainder(1 + size * i, size))
            coarser.src[pl.ds(1 + (size // 2) * i, size // 2)] = restrict_whole(rest, number + 3)

        loop(steps[number], start, steps[number])
        loop(steps[number], smooth, steps[number])
        loop(steps[number], lower, steps[number])

    last = whole[-1]
    last.start(1, 4)
    iterate = last.val[pl.ds(1, 4)]
    direction = iterate
    factor = FIRST
    for _ in range(3):
        _, applied = last.operate(last.val, 1, 4)
        following = 1.0 / (2.0 * RATIO - factor)
        rest = last.src[pl.ds(1, 4)] - applied
        direction = (following * factor) * direction + (2.0 * following / HALF) * (last.inv[pl.ds(1, 4)] * rest)
        iterate = iterate + direction
        last.val[pl.ds(1, 4)] = iterate
        factor = following
    coarse, offset = last.val, 1

    for number in (2, 1, 0):
        level = whole[number]
        size = block[number]
        target, shift = ((answers[2], 2), (answers[3], 0), (answers[4], 0))[number]

        def add(i, level=level, size=size, coarse=coarse, offset=offset, number=number):
            part = coarse[pl.ds(offset + (size // 2) * i, size // 2)]
            at = 1 + size * i
            level.val[pl.ds(at, size)] = level.smo[pl.ds(at, size)] + prolong_whole(part, number + 3)

        def correct(i, level=level, size=size):
            level.correct(1 + size * i, size)

        def finish(i, level=level, size=size, target=target, shift=shift):
            target[pl.ds(shift + size * i, size)] = level.finish(1 + size * i, size)

        loop(steps[number], add, steps[number])
        loop(steps[number], correct, steps[number])
        loop(steps[number], finish, steps[number])
        coarse, offset = target, shift

    for pair in range(6):
        parts = []
        for tile in range(3):
            row = 2 * lax.rem(gy - 1 + tile + RING, RING)
            found = answers[2][2 * gz + pair, row // 8]
            found = sub_take(found, lambda s, row=row: lax.rem(row, 8) + s // 4)
            parts.append(lane_take(found, lambda s, l: (s % 2) * 64 + l // 2))
        found = jnp.stack(parts)
        for plane in (2 * pair, 2 * pair + 1):
            two.val[plane] = two.smo[plane] + found
    for at in (1, 6):
        two.correct(at, 5)
    for at in (2, 6):
        answers[1][pl.ds(at, 4)] = two.finish(at, 4)

    def add_one(i):
        for half in (0, 1):
            plane = 1 + 2 * i + half
            parts = []
            for tile in range(8):
                at = tile + 2
                found = sub_take(answers[1][(plane + 4) // 2, at // 4], lambda s, at=at: (at % 4) * 2 + (s // 2) % 2)
                parts.append(lane_take(found, lambda s, l: 64 * (s % 2) + l // 2))
            one.val[plane] = one.smo[plane] + jnp.stack(parts)

    loop(7, add_one, 7)

    def correct_one(i):
        one.correct(2 + 2 * i, 2)

    loop(6, correct_one, 6)

    def finish_one(i):
        answers[0][pl.ds(3 + 2 * i, 2)] = one.finish(3 + 2 * i, 2)

    loop(5, finish_one, 5)

    def add_zero(i):
        parts = []
        for pair in range(10):
            at = pair + 3
            found = sub_take(
                answers[0][i + 3, at // 2],
                lambda s, at=at: (at % 2) * 4 + (s // 4) * 2 + (s % 4) // 2,
            )
            found = lane_take(found, lambda s, l: 64 * (s % 2) + l // 2)
            parts += [found, found]
        added = jnp.stack(parts)
        for plane in (0, 1):
            zero.val[2 * i + plane] = zero.smo[2 * i + plane] + added

    loop(10, add_zero, 5)

    def correct_zero(i):
        for low in (1, 10):
            zero.correct(i + 1, low, 9)

    loop(18, correct_zero, 3)

    stores = []
    for begin, count in ((0, 8), (8, 4), (12, 4)):

        def finish_zero(i, begin=begin):
            for low in (2, 10):
                staged[begin + i, pl.ds(low - 2, 8)] = zero.finish(begin + i + 2, low, 8)

        loop(count, finish_zero, 4)
        planes = pl.ds(begin, count)
        for group, dst in enumerate((both.at[0], both.at[1])):
            for part in range(4):
                copy = pltpu.make_async_copy(
                    staged.at[planes, :, 4 * group + part],
                    dst.at[planes, :, pl.ds(128 * part, 128)],
                    out_sem.at[len(stores)],
                )
                copy.start()
                stores.append(copy)
    for copy in sent:
        copy.wait_send()
    for slot, ref in ((0, whole[0].mob), (1, whole[0].src)):
        settle(ref, far_send.at[slot, 0], 2 * (RING - 1))
        drain(ref, far_send.at[slot, 1])
    for copy in stores:
        copy.wait()


def scratch_shapes():
    shapes = []

    def arrays(planes, tiles, count=11):
        for _ in range(count):
            shapes.append(pltpu.VMEM((planes, tiles, 8, 128), F32))

    arrays(22, 22, 1)
    arrays(20, 20, 10)
    arrays(16, 8)
    arrays(12, 3)
    for planes, tiles in ((34, 4), (18, 2), (10, 1), (6, 1)):
        arrays(planes, tiles)
    arrays(16, 8, 1)
    arrays(12, 3, 1)
    arrays(36, 4, 1)
    arrays(16, 2, 1)
    arrays(8, 1, 1)
    shapes.append(pltpu.VMEM((22, 22, 8, 128), jnp.int32))
    arrays(16, 16, 1)
    shapes.append(pltpu.VMEM((2, 8, 128), F32))
    shapes.append(pltpu.VMEM((2, 8, 128), F32))
    dma = pltpu.SemaphoreType.DMA
    shapes += [dma((12,)), dma((24,)), dma((7, 8)), dma((7, 8)), dma((2, 3)), dma((2, 2)), pltpu.SemaphoreType.REGULAR((3,))]
    return shapes


def per_device(right_side, cotangent, phase):
    shape = jax.ShapeDtypeStruct((2,) + right_side.shape, F32)
    both = pl.pallas_call(
        kernel,
        out_shape=shape,
        in_specs=[pl.BlockSpec(memory_space=pl.ANY)] * 3,
        out_specs=pl.BlockSpec(memory_space=pl.ANY),
        scratch_shapes=scratch_shapes(),
        compiler_params=pltpu.CompilerParams(
            collective_id=0, has_side_effects=True, vmem_limit_bytes=62 * 2**20
        ),
    )(right_side, cotangent, phase)
    return both[0], both[1]


def solution(mesh):
    spec = P("gz", "gy", None)
    return jax.shard_map(
        per_device, mesh=mesh, in_specs=(spec,) * 3, out_specs=(spec,) * 2, check_vma=False
    )
```

```python
import functools

import jax
import jax.numpy as jnp
from jax import lax
from jax.experimental import pallas as pl
from jax.experimental.pallas import tpu as pltpu
from jax.sharding import PartitionSpec as P

MESH = pl.DeviceIdType.MESH
RING = 16
MID = 1.125
HALF = 0.875
RATIO = MID / HALF
FIRST = 1.0 / RATIO
SECOND = 1.0 / (2.0 * RATIO - FIRST)
C1 = SECOND * FIRST
C2 = 2.0 * SECOND / HALF
LIGHT = 1.0
HEAVY = 1.0 / 8.0
AROUND = ((1, 0), (-1, 0), (1, 1), (1, -1), (-1, 1), (-1, -1), (0, 1), (0, -1))
FAR_Z = tuple(range(1, 16))
FAR_Y = tuple(range(1, 16))
F32 = jnp.float32


def flat(values):
    return values.reshape((-1,) + values.shape[-2:])


def sub_iota(shape):
    return lax.broadcasted_iota(jnp.int32, shape, len(shape) - 2)


def lane_iota(shape):
    return lax.broadcasted_iota(jnp.int32, shape, len(shape) - 1)


def sub_take(values, index_of):
    rows = flat(values)
    if rows.shape[0] == 1:
        rows = rows[0]
    index = index_of(sub_iota(rows.shape))
    return jnp.take_along_axis(rows, index, axis=rows.ndim - 2).reshape(values.shape)


def lane_take(values, index_of):
    rows = flat(values)
    if rows.shape[0] == 1:
        rows = rows[0]
    index = index_of(sub_iota(rows.shape), lane_iota(rows.shape))
    return jnp.take_along_axis(rows, index, axis=rows.ndim - 1).reshape(values.shape)


def sub_roll(values, shift):
    rows = flat(values)
    return pltpu.roll(rows, shift % 8, 1).reshape(values.shape)


def lane_roll(values, shift):
    rows = flat(values)
    return pltpu.roll(rows, shift % 128, 2).reshape(values.shape)


class Level:
    def __init__(self, depth, refs):
        self.depth = depth
        self.scale = 0.5 * 0.25**depth
        self.mob, self.src, self.az, self.ay, self.ax, self.bx, self.inv, self.val, self.smo, self.err, self.rem = refs

    def field_one(self, shape):
        if self.depth == 0:
            return sub_iota(shape) >= 4
        if self.depth == 1:
            return (sub_iota(shape) // 2) % 2 == 1
        if self.depth == 2:
            return sub_iota(shape) % 2 == 1
        return lane_iota(shape) >= 64

    def x_side(self, values, step):
        if self.depth <= 2:
            rolled = lane_roll(values, -step)
            if self.depth == 2:
                return rolled
            if self.depth == 0:
                other = sub_take(rolled, lambda s: (s // 4) * 4 + (s + step + 4) % 4)
            else:
                other = sub_take(rolled, lambda s: s + 1 - 2 * (s % 2))
            edge = 127 if step == 1 else 0
            return jnp.where(lane_iota(values.shape) == edge, other, rolled)
        wide = 2 ** (self.depth - 3)
        return lane_take(values, lambda s, l: (l // 64) * 64 + (l + step * wide + 64) % 64)

    def y_side(self, values, step):
        rows = {1: 4, 2: 2}.get(self.depth, 1)
        count = values.shape[1]
        if count == 1:
            other = values
        elif step == 1:
            other = jnp.concatenate([values[:, 1:], values[:, :1]], axis=1)
        else:
            other = jnp.concatenate([values[:, -1:], values[:, :-1]], axis=1)
        place = sub_iota(values.shape)
        edge = place < rows if step == 1 else place >= 8 - rows
        return sub_roll(jnp.where(edge, other, values), -step * rows)

    def coefficients(self, at, count, mask=None):
        here = self.mob[pl.ds(at, count)]
        up = self.scale * (here + self.mob[pl.ds(at + 1, count)])
        down = self.scale * (here + self.mob[pl.ds(at - 1, count)])
        right = self.scale * (here + self.y_side(here, 1))
        ahead = self.scale * (here + self.x_side(here, 1))
        behind = self.scale * (here + self.x_side(here, -1))
        diagonal = up + down + right + self.y_side(right, -1) + ahead + behind
        self.az[pl.ds(at, count)] = up
        self.ay[pl.ds(at, count)] = right
        self.ax[pl.ds(at, count)] = ahead
        self.bx[pl.ds(at, count)] = behind
        return self.masked_inverse(diagonal, mask)

    def masked_inverse(self, diagonal, mask):
        if mask is None:
            return 1.0 / diagonal
        return mask / (diagonal + (1.0 - mask))

    def operate(self, ref, at, count):
        here = ref[pl.ds(at, count)]
        total = self.az[pl.ds(at, count)] * (here - ref[pl.ds(at + 1, count)])
        total = total + self.az[pl.ds(at - 1, count)] * (here - ref[pl.ds(at - 1, count)])
        flux = self.ay[pl.ds(at, count)] * (here - self.y_side(here, 1))
        total = total + (flux - self.y_side(flux, -1))
        total = total + self.ax[pl.ds(at, count)] * (here - self.x_side(here, 1))
        return here, total + self.bx[pl.ds(at, count)] * (here - self.x_side(here, -1))

    def start(self, at, count):
        self.val[pl.ds(at, count)] = self.src[pl.ds(at, count)] * self.inv[pl.ds(at, count)] * (1.0 / MID)

    def smooth(self, at, count):
        here, applied = self.operate(self.val, at, count)
        rest = self.src[pl.ds(at, count)] - applied
        second = here + C1 * here + C2 * (self.inv[pl.ds(at, count)] * rest)
        self.smo[pl.ds(at, count)] = jnp.where(self.field_one(here.shape), here, second)

    def remainder(self, at, count):
        _, applied = self.operate(self.smo, at, count)
        return self.src[pl.ds(at, count)] - applied

    def correct(self, at, count):
        _, applied = self.operate(self.val, at, count)
        rest = self.src[pl.ds(at, count)] - applied
        self.rem[pl.ds(at, count)] = rest
        self.err[pl.ds(at, count)] = rest * self.inv[pl.ds(at, count)] * (1.0 / MID)

    def finish(self, at, count):
        here, applied = self.operate(self.err, at, count)
        rest = self.rem[pl.ds(at, count)] - applied
        second = C1 * here + C2 * (self.inv[pl.ds(at, count)] * rest)
        base = self.val[pl.ds(at, count)] + here
        return jnp.where(self.field_one(here.shape), base + second, base)


class Finest(Level):
    def coefficients(self, plane, low, count, mask):
        here = self.mob[plane + 1, pl.ds(low, count + 2)]
        mid = here[1:-1]
        up = self.scale * (mid + self.mob[plane + 2, pl.ds(low + 1, count)])
        down = self.scale * (mid + self.mob[plane, pl.ds(low + 1, count)])
        right = self.scale * (here[:-1] + here[1:])
        ahead = self.scale * (mid + self.x_side(mid, 1))
        behind = self.scale * (mid + self.x_side(mid, -1))
        diagonal = up + down + right[1:] + right[:-1] + ahead + behind
        self.az[plane, pl.ds(low, count)] = up
        self.ay[plane, pl.ds(low, count)] = right[1:]
        self.ax[plane, pl.ds(low, count)] = ahead
        self.bx[plane, pl.ds(low, count)] = behind
        inverse = self.masked_inverse(diagonal, mask)
        self.inv[plane, pl.ds(low, count)] = inverse
        self.val[plane, pl.ds(low, count)] = self.src[plane, pl.ds(low, count)] * inverse * (1.0 / MID)

    def operate(self, ref, plane, low, count):
        wide = ref[plane, pl.ds(low - 1, count + 2)]
        here = wide[1:-1]
        part = pl.ds(low, count)
        total = self.az[plane, part] * (here - ref[plane + 1, part])
        total = total + self.az[plane - 1, part] * (here - ref[plane - 1, part])
        flux = self.ay[plane, pl.ds(low - 1, count + 1)] * (wide[:-1] - wide[1:])
        total = total + (flux[1:] - flux[:-1])
        total = total + self.ax[plane, part] * (here - self.x_side(here, 1))
        return here, total + self.bx[plane, part] * (here - self.x_side(here, -1))

    def smooth(self, plane, low, count):
        part = pl.ds(low, count)
        here, applied = self.operate(self.val, plane, low, count)
        rest = self.src[plane, part] - applied
        second = here + C1 * here + C2 * (self.inv[plane, part] * rest)
        self.smo[plane, part] = jnp.where(self.field_one(here.shape), here, second)

    def remainder(self, plane, low, count):
        _, applied = self.operate(self.smo, plane, low, count)
        return self.src[plane, pl.ds(low, count)] - applied

    def correct(self, plane, low, count):
        part = pl.ds(low, count)
        _, applied = self.operate(self.val, plane, low, count)
        rest = self.src[plane, part] - applied
        self.rem[plane, part] = rest
        self.err[plane, part] = rest * self.inv[plane, part] * (1.0 / MID)

    def finish(self, plane, low, count):
        part = pl.ds(low, count)
        here, applied = self.operate(self.err, plane, low, count)
        rest = self.rem[plane, part] - applied
        second = C1 * here + C2 * (self.inv[plane, part] * rest)
        base = self.val[plane, part] + here
        return jnp.where(self.field_one(here.shape), base + second, base)


def halves(values):
    return lane_take(values, lambda s, l: (2 * l) % 128) + lane_take(values, lambda s, l: (2 * l + 1) % 128)


def restrict_0(planes):
    count = planes.shape[0] // 4
    four = planes.reshape((count, 4) + planes.shape[1:])
    out = []
    for pair in (0, 2):
        got = halves(four[:, pair] + four[:, pair + 1])
        left = sub_take(got, lambda s: ((s // 2) % 2) * 4 + 2 * (s % 2))
        right = sub_take(got, lambda s: ((s // 2) % 2) * 4 + 2 * (s % 2) + 1)
        out.append(jnp.where(lane_iota(got.shape) < 64, left, right))
    return 0.125 * jnp.where(sub_iota(out[0].shape) < 4, out[0], out[1])


def restrict_1(planes):
    got = halves(planes + sub_roll(planes, 4))
    left = sub_take(got, lambda s: (s % 2) * 2)
    right = sub_take(got, lambda s: (s % 2) * 2 + 1)
    both = jnp.where(lane_iota(got.shape) < 64, left, right)
    row = sub_iota(both[:, 0].shape) // 2
    out = jnp.where(row == 0, both[:, 0], both[:, 1])
    out = jnp.where(row == 2, both[:, 2], out)
    return 0.125 * jnp.where(row == 3, both[:, 3], out)


def restrict_2(planes):
    got = halves(planes + sub_roll(planes, -2))
    left = sub_take(got, lambda s: (4 * s) % 8)
    right = sub_take(got, lambda s: (4 * s + 1) % 8)
    return 0.125 * jnp.where(lane_iota(got.shape) < 64, left, right)


def restrict_whole(planes, depth):
    wide = 2 ** (depth - 3)
    got = planes + lane_take(planes, lambda s, l: l + wide - 2 * wide * ((l // wide) % 2))
    got = sub_take(got + sub_roll(got, -1), lambda s: (2 * s) % 8)
    count = got.shape[1]
    if count == 1:
        return 0.125 * got
    pairs = got.reshape((got.shape[0], count // 2, 2, 8, 128))
    low = sub_iota(pairs[:, :, 0].shape) < 4
    return 0.125 * jnp.where(low, pairs[:, :, 0], pairs[:, :, 1])


def pair_sum(planes):
    pairs = planes.reshape((planes.shape[0] // 2, 2) + planes.shape[1:])
    return pairs[:, 0] + pairs[:, 1]


def twice(planes):
    shape = (planes.shape[0], 2) + planes.shape[1:]
    return jnp.broadcast_to(planes[:, None], shape).reshape((2 * planes.shape[0],) + planes.shape[1:])


def prolong_whole(coarse, depth):
    if depth == 5:
        return twice(sub_take(coarse, lambda s: s // 2))
    low = sub_take(coarse, lambda s: s // 2)
    high = sub_take(coarse, lambda s: 4 + s // 2)
    both = jnp.stack([low, high], axis=2)
    return twice(both.reshape((coarse.shape[0], 2 * coarse.shape[1], 8, 128)))


def loop(count, body, unroll=1):
    def step(i, carry):
        body(i)
        return carry

    lax.fori_loop(0, count, step, 0, unroll=unroll)


def kernel(rhs, cot, phase, both, *scratch):
    scratch = list(scratch)

    def take(count):
        got = scratch[:count]
        del scratch[:count]
        return got

    zero = Finest(0, take(11))
    one, two = Level(1, take(11)), Level(2, take(11))
    whole = [Level(depth, take(11)) for depth in range(3, 7)]
    answers = take(5)
    phases, staged, rows_m, rows_s = take(4)
    in_sem, out_sem, near_send, near_recv, far_send, far_recv, known = take(7)
    gy, gz = lax.axis_index("gy"), lax.axis_index("gz")

    def to_z(step):
        return {"gz": lax.rem(gz + step + RING, RING)}

    def to_y(step):
        return {"gy": lax.rem(gy + step + RING, RING)}

    def to(dy, dz):
        return {"gy": lax.rem(gy + dy + RING, RING), "gz": lax.rem(gz + dz + RING, RING)}

    barrier = pltpu.get_barrier_semaphore()
    for dy, dz in AROUND:
        pl.semaphore_signal(barrier, inc=1, device_id=to(dy, dz), device_id_type=MESH)

    loads = []
    for group, (src, dst, first) in enumerate(((phase, phases, 0), (rhs, zero.src, 0), (cot, zero.src, 4))):
        edge = 3 if group == 0 else 2
        parts = []
        for part in range(4):
            copy = pltpu.make_async_copy(
                src.at[:, :, pl.ds(128 * part, 128)],
                dst.at[pl.ds(edge, 16), pl.ds(edge, 16), first + part],
                in_sem.at[4 * group + part],
            )
            copy.start()
            parts.append(copy)
        loads.append(parts)


    for level in whole:
        count = level.val.shape[0]
        blank = jnp.zeros((1,) + level.val.shape[1:], F32)
        for ref in (level.mob, level.val, level.smo, level.err):
            ref[pl.ds(0, 1)] = blank
            ref[pl.ds(count - 1, 1)] = blank
    for level in whole:
        level.az[pl.ds(0, 1)] = jnp.zeros((1,) + level.val.shape[1:], F32)
    for end in (0, 34):
        answers[2][pl.ds(end, 2)] = jnp.zeros((2, 4, 8, 128), F32)

    def inside(position, extent):
        ok = jnp.logical_and(position >= 0, position < extent)
        return jnp.where(ok, 1.0, 0.0).astype(F32)

    def mobility_of(values, mask):
        found = jnp.where(values == 1, HEAVY, LIGHT).astype(F32) * mask
        return sub_take(found, lambda s: s % 4)

    for copy in loads[0]:
        copy.wait()
    pl.semaphore_wait(barrier, len(AROUND))

    def tell(number):
        away = 2**number
        for device in (to_z(away), to_z(-away), to_y(away), to_y(-away)):
            pl.semaphore_signal(known.at[number], inc=1, device_id=device, device_id_type=MESH)

    tell(0)

    def edges(step, low, size, width):
        if step == 0:
            return low, low, size
        if step == 1:
            return low + size - width, low - width, width
        return low, low + size, width

    def exchange(slot, ref, z_geometry, y_geometry, rows=None, corner=None):
        copies = []
        for number, (dy, dz) in enumerate(AROUND):
            both = corner is not None and dy != 0 and dz != 0
            z_from, z_to, z_count = edges(dz, *(z_geometry[:2] + (corner,) if both else z_geometry))
            y_from, y_to, y_count = edges(dy, *(y_geometry[:2] + (corner,) if both else y_geometry))
            src = (pl.ds(z_from, z_count), pl.ds(y_from, y_count))
            dst = (pl.ds(z_to, z_count), pl.ds(y_to, y_count))
            if rows is not None:
                src, dst = src + (pl.ds(0, rows),), dst + (pl.ds(0, rows),)
            copy = pltpu.make_async_remote_copy(
                src_ref=ref.at[src],
                dst_ref=ref.at[dst],
                send_sem=near_send.at[slot, number],
                recv_sem=near_recv.at[slot, number],
                device_id=to(dy, dz),
                device_id_type=MESH,
            )
            copy.start()
            copies.append(copy)
        return copies

    def landed(copies):
        for copy in copies:
            copy.wait_recv()

    def place(ref):
        return ref.at[pl.ds(2 * gz + 1, 2), gy // 4, pl.ds(2 * lax.rem(gy, 4), 2)]

    def gather_z(slot, rows, ref):
        own = pltpu.make_async_copy(rows.at[pl.ds(0, 2), pl.ds(0, 2)], place(ref), far_send.at[slot, 2])
        own.start()

        for away in FAR_Z:
            pltpu.make_async_remote_copy(
                src_ref=rows.at[pl.ds(0, 2), pl.ds(0, 2)],
                dst_ref=place(ref),
                send_sem=far_send.at[slot, 0],
                recv_sem=far_recv.at[slot, 0],
                device_id=to_z(away),
                device_id_type=MESH,
            ).start()
        return own

    def settle(ref, semaphore, planes):
        part = ref.at[pl.ds(1, planes), 0, pl.ds(0, 2)]
        pltpu.make_async_copy(part, part, semaphore).wait()

    def gather_y(slot, ref, own):
        own.wait()
        settle(ref, far_recv.at[slot, 0], 2 * (RING - 1))
        part = ref.at[pl.ds(1, 32), gy // 4, pl.ds(2 * lax.rem(gy, 4), 2)]

        for away in FAR_Y:
            pltpu.make_async_remote_copy(
                src_ref=part,
                dst_ref=part,
                send_sem=far_send.at[slot, 1],
                recv_sem=far_recv.at[slot, 1],
                device_id=to_y(away),
                device_id_type=MESH,
            ).start()

    def drain(ref, semaphore):
        part = ref.at[pl.ds(1, 30)]
        pltpu.make_async_copy(part, part, semaphore).wait()

    sent = []
    phase_halo = exchange(0, phases, (3, 16, 3), (3, 16, 3), 4, 2)
    for copy in loads[1] + loads[2]:
        copy.wait()
    source_halo = exchange(1, zero.src, (2, 16, 2), (2, 16, 2), None, 1)
    def own_mobility(i):
        total = None
        for plane in (0, 1):
            at = 3 + 2 * i + plane
            found = mobility_of(phases[at, pl.ds(3, 16)], 1.0)
            zero.mob[at, pl.ds(3, 16)] = found
            total = found if total is None else total + found
        one.mob[4 + i, pl.ds(2, 4)] = restrict_0(total)

    loop(8, own_mobility, 2)
    two.mob[pl.ds(4, 4), 1] = restrict_1(pair_sum(one.mob[pl.ds(4, 8), pl.ds(2, 4)]))
    rows_m[...] = restrict_2(pair_sum(two.mob[pl.ds(4, 4), 1]))
    mob_one = exchange(2, one.mob, (4, 8, 4), (2, 4, 2))
    mob_two = exchange(3, two.mob, (4, 4, 4), (1, 1, 1))
    sent += phase_halo + source_halo + mob_one + mob_two

    def z_mask(plane_at, depth, first):
        block = 16 >> depth
        return inside(gz * block + plane_at - first, 256 >> depth)

    pl.semaphore_wait(known.at[0], 4)
    tell(1)

    def inner_coefficients(i):
        zero.coefficients(3 + i, 3, 14, None)

    loop(14, inner_coefficients, 2)
    pl.semaphore_wait(known.at[1], 4)
    tell(2)

    def inner_smooth(i):
        zero.smooth(4 + i, 4, 12)

    loop(12, inner_smooth, 3)
    pl.semaphore_wait(known.at[2], 4)
    own_m = gather_z(0, rows_m, whole[0].mob)
    landed(phase_halo)

    def outer_mobility(i):
        at = jnp.where(i < 3, i, i + 16)
        mask = z_mask(at, 0, 3)
        zero.mob[at, pl.ds(0, 22)] = mobility_of(phases[at, pl.ds(0, 22)], mask)

    loop(6, outer_mobility, 2)

    def side_mobility(i):
        for first in (0, 19):
            zero.mob[3 + i, pl.ds(first, 3)] = mobility_of(phases[3 + i, pl.ds(first, 3)], 1.0)

    loop(16, side_mobility, 4)

    landed(source_halo)

    def outer_coefficients(i):
        at = jnp.where(i < 3, i, i + 14)
        zero.coefficients(at, 0, 20, z_mask(at, 0, 2))

    loop(6, outer_coefficients, 2)

    def side_coefficients(i):
        for low in (0, 17):
            zero.coefficients(3 + i, low, 3, None)

    loop(14, side_coefficients, 7)

    def outer_smooth(i):
        zero.smooth(jnp.where(i < 3, i + 1, i + 13), 1, 18)

    loop(6, outer_smooth, 2)

    def side_smooth(i):
        for low in (1, 16):
            zero.smooth(4 + i, low, 3)

    loop(12, side_smooth, 6)

    for at in (0, 19):
        zero.smo[at] = zero.val[at]

    def ring_zero(i):
        for at in (0, 19):
            zero.smo[i + 1, at] = zero.val[i + 1, at]

    loop(18, ring_zero, 6)

    def remainder_zero(i):
        for half in (0, 1):
            low = 2 + 8 * half
            total = zero.remainder(2 + 2 * i, low, 8) + zero.remainder(3 + 2 * i, low, 8)
            one.src[4 + i, pl.ds(2 + 2 * half, 2)] = restrict_0(total)

    loop(8, remainder_zero, 4)
    source_one = exchange(4, one.src, (4, 8, 3), (2, 4, 2))
    sent += source_one

    landed(mob_one)
    landed(mob_two)

    def fix_mobility(level, planes, depth):
        for at in range(planes):
            level.mob[at] = level.mob[at] * z_mask(at, depth, planes)
            last = level.mob.shape[0] - 1 - at
            level.mob[last] = level.mob[last] * z_mask(last, depth, planes)

    fix_mobility(one, 4, 1)
    fix_mobility(two, 4, 2)

    def masks(at, count, depth, first):
        return jnp.stack([jnp.full((1, 8, 128), z_mask(at + j, depth, first), F32) for j in range(count)])

    def coefficients_one(i):
        at = 1 + 2 * i
        one.inv[pl.ds(at, 2)] = one.coefficients(at, 2, masks(at, 2, 1, 4))

    loop(7, coefficients_one, 7)

    def coefficients_two(i):
        at = 1 + 2 * i
        found = two.coefficients(at, 2, masks(at, 2, 2, 4))
        two.rem[pl.ds(at, 2)] = found

    loop(5, coefficients_two, 5)
    two.az[0] = two.scale * (two.mob[0] + two.mob[1])
    two.inv[pl.ds(4, 4), 1] = two.rem[pl.ds(4, 4), 1]
    inverse_two = exchange(5, two.inv, (4, 4, 4), (1, 1, 1))
    sent += inverse_two

    landed(source_one)

    def start_one(i):
        one.start(1 + 2 * i, 2)

    loop(7, start_one, 7)

    def smooth_one(i):
        one.smooth(2 + 2 * i, 2)

    loop(6, smooth_one, 6)
    for at in (1, 14):
        one.smo[at] = one.val[at]

    def remainder_one(i):
        rest = one.remainder(4 + 2 * i, 2)[:, 2:6]
        two.src[pl.ds(4 + i, 1), 1] = restrict_1(pair_sum(rest))[0:1]

    loop(4, remainder_one, 4)
    source_two = exchange(6, two.src, (4, 4, 4), (1, 1, 1))
    sent += source_two

    landed(inverse_two)
    for at in (0, 1, 2, 3, 8, 9, 10, 11):
        two.inv[at] = two.inv[at] * z_mask(at, 2, 4)
    landed(source_two)
    for at in (0, 4, 8):
        two.start(at, 4)
    two.smooth(2, 4)
    two.smooth(6, 4)
    for at in (0, 1, 10, 11):
        two.smo[at] = two.val[at]
    rows_s[...] = restrict_2(pair_sum(two.remainder(4, 4)[:, 1]))
    own_s = gather_z(1, rows_s, whole[0].src)
    gather_y(0, whole[0].mob, own_m)

    gather_y(1, whole[0].src, own_s)

    drain(whole[0].mob, far_recv.at[0, 1])

    block = (4, 8, 8, 4)
    steps = (8, 2, 1, 1)
    for number, level in enumerate(whole):
        size = block[number]
        if number > 0:
            finer = whole[number - 1]

            def coarsen(i, finer=finer, level=level, size=size, number=number):
                total = pair_sum(finer.mob[pl.ds(1 + 2 * size * i, 2 * size)])
                level.mob[pl.ds(1 + size * i, size)] = restrict_whole(total, number + 2)

            loop(steps[number], coarsen, steps[number])

        level.az[pl.ds(0, 1)] = level.scale * level.mob[pl.ds(1, 1)]

        def coefficients(i, level=level, size=size):
            at = 1 + size * i
            level.inv[pl.ds(at, size)] = level.coefficients(at, size)

        loop(steps[number], coefficients, steps[number])

    drain(whole[0].src, far_recv.at[1, 1])

    for number, level in enumerate(whole[:-1]):
        size = block[number]
        coarser = whole[number + 1]

        def start(i, level=level, size=size):
            level.start(1 + size * i, size)

        def smooth(i, level=level, size=size):
            level.smooth(1 + size * i, size)

        def lower(i, level=level, size=size, coarser=coarser, number=number):
            rest = pair_sum(level.remainder(1 + size * i, size))
            coarser.src[pl.ds(1 + (size // 2) * i, size // 2)] = restrict_whole(rest, number + 3)

        loop(steps[number], start, steps[number])
        loop(steps[number], smooth, steps[number])
        loop(steps[number], lower, steps[number])

    last = whole[-1]
    last.start(1, 4)
    iterate = last.val[pl.ds(1, 4)]
    direction = iterate
    factor = FIRST
    for _ in range(3):
        _, applied = last.operate(last.val, 1, 4)
        following = 1.0 / (2.0 * RATIO - factor)
        rest = last.src[pl.ds(1, 4)] - applied
        direction = (following * factor) * direction + (2.0 * following / HALF) * (last.inv[pl.ds(1, 4)] * rest)
        iterate = iterate + direction
        last.val[pl.ds(1, 4)] = iterate
        factor = following
    coarse, offset = last.val, 1

    for number in (2, 1, 0):
        level = whole[number]
        size = block[number]
        target, shift = ((answers[2], 2), (answers[3], 0), (answers[4], 0))[number]

        def add(i, level=level, size=size, coarse=coarse, offset=offset, number=number):
            part = coarse[pl.ds(offset + (size // 2) * i, size // 2)]
            at = 1 + size * i
            level.val[pl.ds(at, size)] = level.smo[pl.ds(at, size)] + prolong_whole(part, number + 3)

        def correct(i, level=level, size=size):
            level.correct(1 + size * i, size)

        def finish(i, level=level, size=size, target=target, shift=shift):
            target[pl.ds(shift + size * i, size)] = level.finish(1 + size * i, size)

        loop(steps[number], add, steps[number])
        loop(steps[number], correct, steps[number])
        loop(steps[number], finish, steps[number])
        coarse, offset = target, shift

    for pair in range(6):
        parts = []
        for tile in range(3):
            row = 2 * lax.rem(gy - 1 + tile + RING, RING)
            found = answers[2][2 * gz + pair, row // 8]
            found = sub_take(found, lambda s, row=row: lax.rem(row, 8) + s // 4)
            parts.append(lane_take(found, lambda s, l: (s % 2) * 64 + l // 2))
        found = jnp.stack(parts)
        for plane in (2 * pair, 2 * pair + 1):
            two.val[plane] = two.smo[plane] + found
    for at in (1, 6):
        two.correct(at, 5)
    for at in (2, 6):
        answers[1][pl.ds(at, 4)] = two.finish(at, 4)

    def add_one(i):
        for half in (0, 1):
            plane = 1 + 2 * i + half
            parts = []
            for tile in range(8):
                at = tile + 2
                found = sub_take(answers[1][(plane + 4) // 2, at // 4], lambda s, at=at: (at % 4) * 2 + (s // 2) % 2)
                parts.append(lane_take(found, lambda s, l: 64 * (s % 2) + l // 2))
            one.val[plane] = one.smo[plane] + jnp.stack(parts)

    loop(7, add_one, 7)

    def correct_one(i):
        one.correct(2 + 2 * i, 2)

    loop(6, correct_one, 6)

    def finish_one(i):
        answers[0][pl.ds(3 + 2 * i, 2)] = one.finish(3 + 2 * i, 2)

    loop(5, finish_one, 5)

    def add_zero(i):
        parts = []
        for pair in range(10):
            at = pair + 3
            found = sub_take(
                answers[0][i + 3, at // 2],
                lambda s, at=at: (at % 2) * 4 + (s // 4) * 2 + (s % 4) // 2,
            )
            found = lane_take(found, lambda s, l: 64 * (s % 2) + l // 2)
            parts += [found, found]
        added = jnp.stack(parts)
        for plane in (0, 1):
            zero.val[2 * i + plane] = zero.smo[2 * i + plane] + added

    loop(10, add_zero, 5)

    def correct_zero(i):
        for low in (1, 10):
            zero.correct(i + 1, low, 9)

    loop(18, correct_zero, 3)

    stores = []
    for begin, count in ((0, 8), (8, 4), (12, 4)):

        def finish_zero(i, begin=begin):
            for low in (2, 10):
                staged[begin + i, pl.ds(low - 2, 8)] = zero.finish(begin + i + 2, low, 8)

        loop(count, finish_zero, 4)
        planes = pl.ds(begin, count)
        for group, dst in enumerate((both.at[0], both.at[1])):
            for part in range(4):
                copy = pltpu.make_async_copy(
                    staged.at[planes, :, 4 * group + part],
                    dst.at[planes, :, pl.ds(128 * part, 128)],
                    out_sem.at[len(stores)],
                )
                copy.start()
                stores.append(copy)
    for copy in sent:
        copy.wait_send()
    for slot, ref in ((0, whole[0].mob), (1, whole[0].src)):
        settle(ref, far_send.at[slot, 0], 2 * (RING - 1))
        drain(ref, far_send.at[slot, 1])
    for copy in stores:
        copy.wait()


def scratch_shapes():
    shapes = []

    def arrays(planes, tiles, count=11):
        for _ in range(count):
            shapes.append(pltpu.VMEM((planes, tiles, 8, 128), F32))

    arrays(22, 22, 1)
    arrays(20, 20, 10)
    arrays(16, 8)
    arrays(12, 3)
    for planes, tiles in ((34, 4), (18, 2), (10, 1), (6, 1)):
        arrays(planes, tiles)
    arrays(16, 8, 1)
    arrays(12, 3, 1)
    arrays(36, 4, 1)
    arrays(16, 2, 1)
    arrays(8, 1, 1)
    shapes.append(pltpu.VMEM((22, 22, 8, 128), jnp.int32))
    arrays(16, 16, 1)
    shapes.append(pltpu.VMEM((2, 8, 128), F32))
    shapes.append(pltpu.VMEM((2, 8, 128), F32))
    dma = pltpu.SemaphoreType.DMA
    shapes += [dma((12,)), dma((24,)), dma((7, 8)), dma((7, 8)), dma((2, 3)), dma((2, 2)), pltpu.SemaphoreType.REGULAR((3,))]
    return shapes


def per_device(right_side, cotangent, phase):
    shape = jax.ShapeDtypeStruct((2,) + right_side.shape, F32)
    both = pl.pallas_call(
        kernel,
        out_shape=shape,
        in_specs=[pl.BlockSpec(memory_space=pl.ANY)] * 3,
        out_specs=pl.BlockSpec(memory_space=pl.ANY),
        scratch_shapes=scratch_shapes(),
        compiler_params=pltpu.CompilerParams(
            collective_id=0, has_side_effects=True, vmem_limit_bytes=62 * 2**20
        ),
    )(right_side, cotangent, phase)
    return both[0], both[1]


def solution(mesh):
    spec = P("gz", "gy", None)
    return jax.shard_map(
        per_device, mesh=mesh, in_specs=(spec,) * 3, out_specs=(spec,) * 2, check_vma=False
    )
```

```python
import functools

import jax
import jax.numpy as jnp
from jax import lax
from jax.experimental import pallas as pl
from jax.experimental.pallas import tpu as pltpu
from jax.sharding import PartitionSpec as P

MESH = pl.DeviceIdType.MESH
RING = 16
MID = 1.125
HALF = 0.875
RATIO = MID / HALF
FIRST = 1.0 / RATIO
SECOND = 1.0 / (2.0 * RATIO - FIRST)
C1 = SECOND * FIRST
C2 = 2.0 * SECOND / HALF
LIGHT = 1.0
HEAVY = 1.0 / 8.0
AROUND = ((1, 0), (-1, 0), (1, 1), (1, -1), (-1, 1), (-1, -1), (0, 1), (0, -1))
FAR_Z = tuple(range(1, 16))
FAR_Y = tuple(range(1, 16))
F32 = jnp.float32


def flat(values):
    return values.reshape((-1,) + values.shape[-2:])


def sub_iota(shape):
    return lax.broadcasted_iota(jnp.int32, shape, len(shape) - 2)


def lane_iota(shape):
    return lax.broadcasted_iota(jnp.int32, shape, len(shape) - 1)


def sub_take(values, index_of):
    rows = flat(values)
    if rows.shape[0] == 1:
        rows = rows[0]
    index = index_of(sub_iota(rows.shape))
    return jnp.take_along_axis(rows, index, axis=rows.ndim - 2).reshape(values.shape)


def lane_take(values, index_of):
    rows = flat(values)
    if rows.shape[0] == 1:
        rows = rows[0]
    index = index_of(sub_iota(rows.shape), lane_iota(rows.shape))
    return jnp.take_along_axis(rows, index, axis=rows.ndim - 1).reshape(values.shape)


def sub_roll(values, shift):
    rows = flat(values)
    return pltpu.roll(rows, shift % 8, 1).reshape(values.shape)


def lane_roll(values, shift):
    rows = flat(values)
    return pltpu.roll(rows, shift % 128, 2).reshape(values.shape)


class Level:
    def __init__(self, depth, refs):
        self.depth = depth
        self.scale = 0.5 * 0.25**depth
        self.mob, self.src, self.az, self.ay, self.ax, self.bx, self.inv, self.val, self.smo, self.err, self.rem = refs

    def field_one(self, shape):
        if self.depth == 0:
            return sub_iota(shape) >= 4
        if self.depth == 1:
            return (sub_iota(shape) // 2) % 2 == 1
        if self.depth == 2:
            return sub_iota(shape) % 2 == 1
        return lane_iota(shape) >= 64

    def x_side(self, values, step):
        if self.depth <= 2:
            rolled = lane_roll(values, -step)
            if self.depth == 2:
                return rolled
            if self.depth == 0:
                other = sub_take(rolled, lambda s: (s // 4) * 4 + (s + step + 4) % 4)
            else:
                other = sub_take(rolled, lambda s: s + 1 - 2 * (s % 2))
            edge = 127 if step == 1 else 0
            return jnp.where(lane_iota(values.shape) == edge, other, rolled)
        wide = 2 ** (self.depth - 3)
        return lane_take(values, lambda s, l: (l // 64) * 64 + (l + step * wide + 64) % 64)

    def y_side(self, values, step):
        rows = {1: 4, 2: 2}.get(self.depth, 1)
        count = values.shape[1]
        if count == 1:
            other = values
        elif step == 1:
            other = jnp.concatenate([values[:, 1:], values[:, :1]], axis=1)
        else:
            other = jnp.concatenate([values[:, -1:], values[:, :-1]], axis=1)
        place = sub_iota(values.shape)
        edge = place < rows if step == 1 else place >= 8 - rows
        return sub_roll(jnp.where(edge, other, values), -step * rows)

    def coefficients(self, at, count, mask=None):
        here = self.mob[pl.ds(at, count)]
        up = self.scale * (here + self.mob[pl.ds(at + 1, count)])
        down = self.scale * (here + self.mob[pl.ds(at - 1, count)])
        right = self.scale * (here + self.y_side(here, 1))
        ahead = self.scale * (here + self.x_side(here, 1))
        behind = self.scale * (here + self.x_side(here, -1))
        diagonal = up + down + right + self.y_side(right, -1) + ahead + behind
        self.az[pl.ds(at, count)] = up
        self.ay[pl.ds(at, count)] = right
        self.ax[pl.ds(at, count)] = ahead
        self.bx[pl.ds(at, count)] = behind
        return self.masked_inverse(diagonal, mask)

    def masked_inverse(self, diagonal, mask):
        if mask is None:
            return 1.0 / diagonal
        return mask / (diagonal + (1.0 - mask))

    def operate(self, ref, at, count):
        here = ref[pl.ds(at, count)]
        total = self.az[pl.ds(at, count)] * (here - ref[pl.ds(at + 1, count)])
        total = total + self.az[pl.ds(at - 1, count)] * (here - ref[pl.ds(at - 1, count)])
        flux = self.ay[pl.ds(at, count)] * (here - self.y_side(here, 1))
        total = total + (flux - self.y_side(flux, -1))
        total = total + self.ax[pl.ds(at, count)] * (here - self.x_side(here, 1))
        return here, total + self.bx[pl.ds(at, count)] * (here - self.x_side(here, -1))

    def start(self, at, count):
        self.val[pl.ds(at, count)] = self.src[pl.ds(at, count)] * self.inv[pl.ds(at, count)] * (1.0 / MID)

    def smooth(self, at, count):
        here, applied = self.operate(self.val, at, count)
        rest = self.src[pl.ds(at, count)] - applied
        second = here + C1 * here + C2 * (self.inv[pl.ds(at, count)] * rest)
        self.smo[pl.ds(at, count)] = jnp.where(self.field_one(here.shape), here, second)

    def remainder(self, at, count):
        _, applied = self.operate(self.smo, at, count)
        return self.src[pl.ds(at, count)] - applied

    def correct(self, at, count):
        _, applied = self.operate(self.val, at, count)
        rest = self.src[pl.ds(at, count)] - applied
        self.rem[pl.ds(at, count)] = rest
        self.err[pl.ds(at, count)] = rest * self.inv[pl.ds(at, count)] * (1.0 / MID)

    def finish(self, at, count):
        here, applied = self.operate(self.err, at, count)
        rest = self.rem[pl.ds(at, count)] - applied
        second = C1 * here + C2 * (self.inv[pl.ds(at, count)] * rest)
        base = self.val[pl.ds(at, count)] + here
        return jnp.where(self.field_one(here.shape), base + second, base)


class Finest(Level):
    def coefficients(self, plane, low, count, mask):
        here = self.mob[plane + 1, pl.ds(low, count + 2)]
        mid = here[1:-1]
        up = self.scale * (mid + self.mob[plane + 2, pl.ds(low + 1, count)])
        down = self.scale * (mid + self.mob[plane, pl.ds(low + 1, count)])
        right = self.scale * (here[:-1] + here[1:])
        ahead = self.scale * (mid + self.x_side(mid, 1))
        behind = self.scale * (mid + self.x_side(mid, -1))
        diagonal = up + down + right[1:] + right[:-1] + ahead + behind
        self.az[plane, pl.ds(low, count)] = up
        self.ay[plane, pl.ds(low, count)] = right[1:]
        self.ax[plane, pl.ds(low, count)] = ahead
        self.bx[plane, pl.ds(low, count)] = behind
        inverse = self.masked_inverse(diagonal, mask)
        self.inv[plane, pl.ds(low, count)] = inverse
        self.val[plane, pl.ds(low, count)] = self.src[plane, pl.ds(low, count)] * inverse * (1.0 / MID)

    def operate(self, ref, plane, low, count):
        wide = ref[plane, pl.ds(low - 1, count + 2)]
        here = wide[1:-1]
        part = pl.ds(low, count)
        total = self.az[plane, part] * (here - ref[plane + 1, part])
        total = total + self.az[plane - 1, part] * (here - ref[plane - 1, part])
        flux = self.ay[plane, pl.ds(low - 1, count + 1)] * (wide[:-1] - wide[1:])
        total = total + (flux[1:] - flux[:-1])
        total = total + self.ax[plane, part] * (here - self.x_side(here, 1))
        return here, total + self.bx[plane, part] * (here - self.x_side(here, -1))

    def smooth(self, plane, low, count):
        part = pl.ds(low, count)
        here, applied = self.operate(self.val, plane, low, count)
        rest = self.src[plane, part] - applied
        second = here + C1 * here + C2 * (self.inv[plane, part] * rest)
        self.smo[plane, part] = jnp.where(self.field_one(here.shape), here, second)

    def remainder(self, plane, low, count):
        _, applied = self.operate(self.smo, plane, low, count)
        return self.src[plane, pl.ds(low, count)] - applied

    def correct(self, plane, low, count):
        part = pl.ds(low, count)
        _, applied = self.operate(self.val, plane, low, count)
        rest = self.src[plane, part] - applied
        self.rem[plane, part] = rest
        self.err[plane, part] = rest * self.inv[plane, part] * (1.0 / MID)

    def finish(self, plane, low, count):
        part = pl.ds(low, count)
        here, applied = self.operate(self.err, plane, low, count)
        rest = self.rem[plane, part] - applied
        second = C1 * here + C2 * (self.inv[plane, part] * rest)
        base = self.val[plane, part] + here
        return jnp.where(self.field_one(here.shape), base + second, base)


def halves(values):
    return lane_take(values, lambda s, l: (2 * l) % 128) + lane_take(values, lambda s, l: (2 * l + 1) % 128)


def restrict_0(planes):
    count = planes.shape[0] // 4
    four = planes.reshape((count, 4) + planes.shape[1:])
    out = []
    for pair in (0, 2):
        got = halves(four[:, pair] + four[:, pair + 1])
        left = sub_take(got, lambda s: ((s // 2) % 2) * 4 + 2 * (s % 2))
        right = sub_take(got, lambda s: ((s // 2) % 2) * 4 + 2 * (s % 2) + 1)
        out.append(jnp.where(lane_iota(got.shape) < 64, left, right))
    return 0.125 * jnp.where(sub_iota(out[0].shape) < 4, out[0], out[1])


def restrict_1(planes):
    got = halves(planes + sub_roll(planes, 4))
    left = sub_take(got, lambda s: (s % 2) * 2)
    right = sub_take(got, lambda s: (s % 2) * 2 + 1)
    both = jnp.where(lane_iota(got.shape) < 64, left, right)
    row = sub_iota(both[:, 0].shape) // 2
    out = jnp.where(row == 0, both[:, 0], both[:, 1])
    out = jnp.where(row == 2, both[:, 2], out)
    return 0.125 * jnp.where(row == 3, both[:, 3], out)


def restrict_2(planes):
    got = halves(planes + sub_roll(planes, -2))
    left = sub_take(got, lambda s: (4 * s) % 8)
    right = sub_take(got, lambda s: (4 * s + 1) % 8)
    return 0.125 * jnp.where(lane_iota(got.shape) < 64, left, right)


def restrict_whole(planes, depth):
    wide = 2 ** (depth - 3)
    got = planes + lane_take(planes, lambda s, l: l + wide - 2 * wide * ((l // wide) % 2))
    got = sub_take(got + sub_roll(got, -1), lambda s: (2 * s) % 8)
    count = got.shape[1]
    if count == 1:
        return 0.125 * got
    pairs = got.reshape((got.shape[0], count // 2, 2, 8, 128))
    low = sub_iota(pairs[:, :, 0].shape) < 4
    return 0.125 * jnp.where(low, pairs[:, :, 0], pairs[:, :, 1])


def pair_sum(planes):
    pairs = planes.reshape((planes.shape[0] // 2, 2) + planes.shape[1:])
    return pairs[:, 0] + pairs[:, 1]


def twice(planes):
    shape = (planes.shape[0], 2) + planes.shape[1:]
    return jnp.broadcast_to(planes[:, None], shape).reshape((2 * planes.shape[0],) + planes.shape[1:])


def prolong_whole(coarse, depth):
    if depth == 5:
        return twice(sub_take(coarse, lambda s: s // 2))
    low = sub_take(coarse, lambda s: s // 2)
    high = sub_take(coarse, lambda s: 4 + s // 2)
    both = jnp.stack([low, high], axis=2)
    return twice(both.reshape((coarse.shape[0], 2 * coarse.shape[1], 8, 128)))


def loop(count, body, unroll=1):
    def step(i, carry):
        body(i)
        return carry

    lax.fori_loop(0, count, step, 0, unroll=unroll)


def kernel(rhs, cot, phase, both, *scratch):
    scratch = list(scratch)

    def take(count):
        got = scratch[:count]
        del scratch[:count]
        return got

    zero = Finest(0, take(11))
    one, two = Level(1, take(11)), Level(2, take(11))
    whole = [Level(depth, take(11)) for depth in range(3, 7)]
    answers = take(5)
    phases, staged, rows_m, rows_s, packed_m = take(5)
    in_sem, out_sem, near_send, near_recv, far_send, far_recv, known = take(7)
    gy, gz = lax.axis_index("gy"), lax.axis_index("gz")

    def to_z(step):
        return {"gz": lax.rem(gz + step + RING, RING)}

    def to_y(step):
        return {"gy": lax.rem(gy + step + RING, RING)}

    def to(dy, dz):
        return {"gy": lax.rem(gy + dy + RING, RING), "gz": lax.rem(gz + dz + RING, RING)}

    barrier = pltpu.get_barrier_semaphore()
    for dy, dz in AROUND:
        pl.semaphore_signal(barrier, inc=1, device_id=to(dy, dz), device_id_type=MESH)

    loads = []
    for group, (src, dst, first) in enumerate(((phase, phases, 0), (rhs, zero.src, 0), (cot, zero.src, 4))):
        edge = 3 if group == 0 else 2
        parts = []
        for part in range(4):
            copy = pltpu.make_async_copy(
                src.at[:, :, pl.ds(128 * part, 128)],
                dst.at[pl.ds(edge, 16), pl.ds(edge, 16), first + part],
                in_sem.at[4 * group + part],
            )
            copy.start()
            parts.append(copy)
        loads.append(parts)


    for level in whole:
        count = level.val.shape[0]
        blank = jnp.zeros((1,) + level.val.shape[1:], F32)
        for ref in (level.mob, level.val, level.smo, level.err):
            ref[pl.ds(0, 1)] = blank
            ref[pl.ds(count - 1, 1)] = blank
    for level in whole:
        level.az[pl.ds(0, 1)] = jnp.zeros((1,) + level.val.shape[1:], F32)
    for end in (0, 34):
        answers[2][pl.ds(end, 2)] = jnp.zeros((2, 4, 8, 128), F32)

    def inside(position, extent):
        ok = jnp.logical_and(position >= 0, position < extent)
        return jnp.where(ok, 1.0, 0.0).astype(F32)

    def mobility_of(values, mask):
        found = jnp.where(values == 1, HEAVY, LIGHT).astype(F32) * mask
        return sub_take(found, lambda s: s % 4)

    for copy in loads[0]:
        copy.wait()
    pl.semaphore_wait(barrier, len(AROUND))

    def tell(number):
        away = 2**number
        for device in (to_z(away), to_z(-away), to_y(away), to_y(-away)):
            pl.semaphore_signal(known.at[number], inc=1, device_id=device, device_id_type=MESH)

    tell(0)

    def edges(step, low, size, width):
        if step == 0:
            return low, low, size
        if step == 1:
            return low + size - width, low - width, width
        return low, low + size, width

    def exchange(slot, ref, z_geometry, y_geometry, rows=None, corner=None):
        copies = []
        for number, (dy, dz) in enumerate(AROUND):
            both = corner is not None and dy != 0 and dz != 0
            z_from, z_to, z_count = edges(dz, *(z_geometry[:2] + (corner,) if both else z_geometry))
            y_from, y_to, y_count = edges(dy, *(y_geometry[:2] + (corner,) if both else y_geometry))
            src = (pl.ds(z_from, z_count), pl.ds(y_from, y_count))
            dst = (pl.ds(z_to, z_count), pl.ds(y_to, y_count))
            if rows is not None:
                src, dst = src + (pl.ds(0, rows),), dst + (pl.ds(0, rows),)
            copy = pltpu.make_async_remote_copy(
                src_ref=ref.at[src],
                dst_ref=ref.at[dst],
                send_sem=near_send.at[slot, number],
                recv_sem=near_recv.at[slot, number],
                device_id=to(dy, dz),
                device_id_type=MESH,
            )
            copy.start()
            copies.append(copy)
        return copies

    def landed(copies):
        for copy in copies:
            copy.wait_recv()

    def place(slot, ref):
        planes = pl.ds(gz, 1) if slot == 0 else pl.ds(2 * gz + 1, 2)
        return ref.at[planes, gy // 4, pl.ds(2 * lax.rem(gy, 4), 2)]

    def gather_z(slot, rows, ref):
        part = rows.at[pl.ds(0, 1 + slot), pl.ds(0, 2)]
        own = pltpu.make_async_copy(part, place(slot, ref), far_send.at[slot, 2])
        own.start()

        for away in FAR_Z:
            pltpu.make_async_remote_copy(
                src_ref=part,
                dst_ref=place(slot, ref),
                send_sem=far_send.at[slot, 0],
                recv_sem=far_recv.at[slot, 0],
                device_id=to_z(away),
                device_id_type=MESH,
            ).start()
        return own

    def settle(ref, semaphore, planes):
        part = ref.at[pl.ds(0, planes), 0, pl.ds(0, 2)]
        pltpu.make_async_copy(part, part, semaphore).wait()

    def gather_y(slot, ref, own):
        own.wait()
        settle(ref, far_recv.at[slot, 0], (1 + slot) * (RING - 1))
        planes = pl.ds(0, 16) if slot == 0 else pl.ds(1, 32)
        part = ref.at[planes, gy // 4, pl.ds(2 * lax.rem(gy, 4), 2)]

        for away in FAR_Y:
            pltpu.make_async_remote_copy(
                src_ref=part,
                dst_ref=part,
                send_sem=far_send.at[slot, 1],
                recv_sem=far_recv.at[slot, 1],
                device_id=to_y(away),
                device_id_type=MESH,
            ).start()

    def drain(slot, ref, semaphore):
        part = ref.at[pl.ds(0, 15 + 15 * slot)]
        pltpu.make_async_copy(part, part, semaphore).wait()

    sent = []
    phase_halo = exchange(0, phases, (3, 16, 3), (3, 16, 3), 4, 2)
    for copy in loads[1] + loads[2]:
        copy.wait()
    source_halo = exchange(1, zero.src, (2, 16, 2), (2, 16, 2), None, 1)
    def own_mobility(i):
        total = None
        for plane in (0, 1):
            at = 3 + 2 * i + plane
            found = mobility_of(phases[at, pl.ds(3, 16)], 1.0)
            zero.mob[at, pl.ds(3, 16)] = found
            total = found if total is None else total + found
        one.mob[4 + i, pl.ds(2, 4)] = restrict_0(total)

    loop(8, own_mobility, 2)
    two.mob[pl.ds(4, 4), 1] = restrict_1(pair_sum(one.mob[pl.ds(4, 8), pl.ds(2, 4)]))
    found = restrict_2(pair_sum(two.mob[pl.ds(4, 4), 1]))
    rows_m[0] = jnp.where(lane_iota((8, 128)) < 64, found[0], found[1])
    mob_one = exchange(2, one.mob, (4, 8, 4), (2, 4, 2))
    mob_two = exchange(3, two.mob, (4, 4, 4), (1, 1, 1))
    sent += phase_halo + source_halo + mob_one + mob_two

    def z_mask(plane_at, depth, first):
        block = 16 >> depth
        return inside(gz * block + plane_at - first, 256 >> depth)

    pl.semaphore_wait(known.at[0], 4)
    tell(1)

    def inner_coefficients(i):
        zero.coefficients(3 + i, 3, 14, None)

    loop(14, inner_coefficients, 2)
    pl.semaphore_wait(known.at[1], 4)
    tell(2)

    def inner_smooth(i):
        zero.smooth(4 + i, 4, 12)

    loop(12, inner_smooth, 3)
    pl.semaphore_wait(known.at[2], 4)
    own_m = gather_z(0, rows_m, packed_m)
    landed(phase_halo)

    def outer_mobility(i):
        at = jnp.where(i < 3, i, i + 16)
        mask = z_mask(at, 0, 3)
        zero.mob[at, pl.ds(0, 22)] = mobility_of(phases[at, pl.ds(0, 22)], mask)

    loop(6, outer_mobility, 2)

    def side_mobility(i):
        for first in (0, 19):
            zero.mob[3 + i, pl.ds(first, 3)] = mobility_of(phases[3 + i, pl.ds(first, 3)], 1.0)

    loop(16, side_mobility, 4)

    landed(source_halo)

    def outer_coefficients(i):
        at = jnp.where(i < 3, i, i + 14)
        zero.coefficients(at, 0, 20, z_mask(at, 0, 2))

    loop(6, outer_coefficients, 2)

    def side_coefficients(i):
        for low in (0, 17):
            zero.coefficients(3 + i, low, 3, None)

    loop(14, side_coefficients, 7)

    def outer_smooth(i):
        zero.smooth(jnp.where(i < 3, i + 1, i + 13), 1, 18)

    loop(6, outer_smooth, 2)

    def side_smooth(i):
        for low in (1, 16):
            zero.smooth(4 + i, low, 3)

    loop(12, side_smooth, 6)

    for at in (0, 19):
        zero.smo[at] = zero.val[at]

    def ring_zero(i):
        for at in (0, 19):
            zero.smo[i + 1, at] = zero.val[i + 1, at]

    loop(18, ring_zero, 6)

    def remainder_zero(i):
        for half in (0, 1):
            low = 2 + 8 * half
            total = zero.remainder(2 + 2 * i, low, 8) + zero.remainder(3 + 2 * i, low, 8)
            one.src[4 + i, pl.ds(2 + 2 * half, 2)] = restrict_0(total)

    loop(8, remainder_zero, 4)
    source_one = exchange(4, one.src, (4, 8, 3), (2, 4, 2))
    sent += source_one

    landed(mob_one)
    landed(mob_two)

    def fix_mobility(level, planes, depth):
        for at in range(planes):
            level.mob[at] = level.mob[at] * z_mask(at, depth, planes)
            last = level.mob.shape[0] - 1 - at
            level.mob[last] = level.mob[last] * z_mask(last, depth, planes)

    fix_mobility(one, 4, 1)
    fix_mobility(two, 4, 2)

    def masks(at, count, depth, first):
        return jnp.stack([jnp.full((1, 8, 128), z_mask(at + j, depth, first), F32) for j in range(count)])

    def coefficients_one(i):
        at = 1 + 2 * i
        one.inv[pl.ds(at, 2)] = one.coefficients(at, 2, masks(at, 2, 1, 4))

    loop(7, coefficients_one, 7)

    def coefficients_two(i):
        at = 1 + 2 * i
        found = two.coefficients(at, 2, masks(at, 2, 2, 4))
        two.rem[pl.ds(at, 2)] = found

    loop(5, coefficients_two, 5)
    two.az[0] = two.scale * (two.mob[0] + two.mob[1])
    two.inv[pl.ds(4, 4), 1] = two.rem[pl.ds(4, 4), 1]
    inverse_two = exchange(5, two.inv, (4, 4, 4), (1, 1, 1))
    sent += inverse_two

    landed(source_one)

    def start_one(i):
        one.start(1 + 2 * i, 2)

    loop(7, start_one, 7)

    def smooth_one(i):
        one.smooth(2 + 2 * i, 2)

    loop(6, smooth_one, 6)
    for at in (1, 14):
        one.smo[at] = one.val[at]

    def remainder_one(i):
        rest = one.remainder(4 + 2 * i, 2)[:, 2:6]
        two.src[pl.ds(4 + i, 1), 1] = restrict_1(pair_sum(rest))[0:1]

    loop(4, remainder_one, 4)
    source_two = exchange(6, two.src, (4, 4, 4), (1, 1, 1))
    sent += source_two

    landed(inverse_two)
    for at in (0, 1, 2, 3, 8, 9, 10, 11):
        two.inv[at] = two.inv[at] * z_mask(at, 2, 4)
    landed(source_two)
    for at in (0, 4, 8):
        two.start(at, 4)
    two.smooth(2, 4)
    two.smooth(6, 4)
    for at in (0, 1, 10, 11):
        two.smo[at] = two.val[at]
    rows_s[...] = restrict_2(pair_sum(two.remainder(4, 4)[:, 1]))
    own_s = gather_z(1, rows_s, whole[0].src)
    gather_y(0, packed_m, own_m)

    gather_y(1, whole[0].src, own_s)

    drain(0, packed_m, far_recv.at[0, 1])

    def unpack(i):
        found = packed_m[pl.ds(2 * i, 2)]
        turned = lane_roll(found, 64)
        low = lane_iota(found.shape) < 64
        pair = jnp.stack([jnp.where(low, found, turned), jnp.where(low, turned, found)], axis=1)
        whole[0].mob[pl.ds(1 + 4 * i, 4)] = pair.reshape((4, 4, 8, 128))

    loop(8, unpack, 4)

    block = (4, 8, 8, 4)
    steps = (8, 2, 1, 1)
    for number, level in enumerate(whole):
        size = block[number]
        if number > 0:
            finer = whole[number - 1]

            def coarsen(i, finer=finer, level=level, size=size, number=number):
                total = pair_sum(finer.mob[pl.ds(1 + 2 * size * i, 2 * size)])
                level.mob[pl.ds(1 + size * i, size)] = restrict_whole(total, number + 2)

            loop(steps[number], coarsen, steps[number])

        level.az[pl.ds(0, 1)] = level.scale * level.mob[pl.ds(1, 1)]

        def coefficients(i, level=level, size=size):
            at = 1 + size * i
            level.inv[pl.ds(at, size)] = level.coefficients(at, size)

        loop(steps[number], coefficients, steps[number])

    drain(1, whole[0].src, far_recv.at[1, 1])

    for number, level in enumerate(whole[:-1]):
        size = block[number]
        coarser = whole[number + 1]

        def start(i, level=level, size=size):
            level.start(1 + size * i, size)

        def smooth(i, level=level, size=size):
            level.smooth(1 + size * i, size)

        def lower(i, level=level, size=size, coarser=coarser, number=number):
            rest = pair_sum(level.remainder(1 + size * i, size))
            coarser.src[pl.ds(1 + (size // 2) * i, size // 2)] = restrict_whole(rest, number + 3)

        loop(steps[number], start, steps[number])
        loop(steps[number], smooth, steps[number])
        loop(steps[number], lower, steps[number])

    last = whole[-1]
    last.start(1, 4)
    iterate = last.val[pl.ds(1, 4)]
    direction = iterate
    factor = FIRST
    for _ in range(3):
        _, applied = last.operate(last.val, 1, 4)
        following = 1.0 / (2.0 * RATIO - factor)
        rest = last.src[pl.ds(1, 4)] - applied
        direction = (following * factor) * direction + (2.0 * following / HALF) * (last.inv[pl.ds(1, 4)] * rest)
        iterate = iterate + direction
        last.val[pl.ds(1, 4)] = iterate
        factor = following
    coarse, offset = last.val, 1

    for number in (2, 1, 0):
        level = whole[number]
        size = block[number]
        target, shift = ((answers[2], 2), (answers[3], 0), (answers[4], 0))[number]

        def add(i, level=level, size=size, coarse=coarse, offset=offset, number=number):
            part = coarse[pl.ds(offset + (size // 2) * i, size // 2)]
            at = 1 + size * i
            level.val[pl.ds(at, size)] = level.smo[pl.ds(at, size)] + prolong_whole(part, number + 3)

        def correct(i, level=level, size=size):
            level.correct(1 + size * i, size)

        def finish(i, level=level, size=size, target=target, shift=shift):
            target[pl.ds(shift + size * i, size)] = level.finish(1 + size * i, size)

        loop(steps[number], add, steps[number])
        loop(steps[number], correct, steps[number])
        loop(steps[number], finish, steps[number])
        coarse, offset = target, shift

    for pair in range(6):
        parts = []
        for tile in range(3):
            row = 2 * lax.rem(gy - 1 + tile + RING, RING)
            found = answers[2][2 * gz + pair, row // 8]
            found = sub_take(found, lambda s, row=row: lax.rem(row, 8) + s // 4)
            parts.append(lane_take(found, lambda s, l: (s % 2) * 64 + l // 2))
        found = jnp.stack(parts)
        for plane in (2 * pair, 2 * pair + 1):
            two.val[plane] = two.smo[plane] + found
    for at in (1, 6):
        two.correct(at, 5)
    for at in (2, 6):
        answers[1][pl.ds(at, 4)] = two.finish(at, 4)

    def add_one(i):
        for half in (0, 1):
            plane = 1 + 2 * i + half
            parts = []
            for tile in range(8):
                at = tile + 2
                found = sub_take(answers[1][(plane + 4) // 2, at // 4], lambda s, at=at: (at % 4) * 2 + (s // 2) % 2)
                parts.append(lane_take(found, lambda s, l: 64 * (s % 2) + l // 2))
            one.val[plane] = one.smo[plane] + jnp.stack(parts)

    loop(7, add_one, 7)

    def correct_one(i):
        one.correct(2 + 2 * i, 2)

    loop(6, correct_one, 6)

    def finish_one(i):
        answers[0][pl.ds(3 + 2 * i, 2)] = one.finish(3 + 2 * i, 2)

    loop(5, finish_one, 5)

    def add_zero(i):
        parts = []
        for pair in range(10):
            at = pair + 3
            found = sub_take(
                answers[0][i + 3, at // 2],
                lambda s, at=at: (at % 2) * 4 + (s // 4) * 2 + (s % 4) // 2,
            )
            found = lane_take(found, lambda s, l: 64 * (s % 2) + l // 2)
            parts += [found, found]
        added = jnp.stack(parts)
        for plane in (0, 1):
            zero.val[2 * i + plane] = zero.smo[2 * i + plane] + added

    loop(10, add_zero, 5)

    def correct_zero(i):
        for low in (1, 10):
            zero.correct(i + 1, low, 9)

    loop(18, correct_zero, 3)

    stores = []
    for begin, count in ((0, 8), (8, 4), (12, 4)):

        def finish_zero(i, begin=begin):
            for low in (2, 10):
                staged[begin + i, pl.ds(low - 2, 8)] = zero.finish(begin + i + 2, low, 8)

        loop(count, finish_zero, 4)
        planes = pl.ds(begin, count)
        for group, dst in enumerate((both.at[0], both.at[1])):
            for part in range(4):
                copy = pltpu.make_async_copy(
                    staged.at[planes, :, 4 * group + part],
                    dst.at[planes, :, pl.ds(128 * part, 128)],
                    out_sem.at[len(stores)],
                )
                copy.start()
                stores.append(copy)
    for copy in sent:
        copy.wait_send()
    for slot, ref in ((0, packed_m), (1, whole[0].src)):
        settle(ref, far_send.at[slot, 0], (1 + slot) * (RING - 1))
        drain(slot, ref, far_send.at[slot, 1])
    for copy in stores:
        copy.wait()


def scratch_shapes():
    shapes = []

    def arrays(planes, tiles, count=11):
        for _ in range(count):
            shapes.append(pltpu.VMEM((planes, tiles, 8, 128), F32))

    arrays(22, 22, 1)
    arrays(20, 20, 10)
    arrays(16, 8)
    arrays(12, 3)
    for planes, tiles in ((34, 4), (18, 2), (10, 1), (6, 1)):
        arrays(planes, tiles)
    arrays(16, 8, 1)
    arrays(12, 3, 1)
    arrays(36, 4, 1)
    arrays(16, 2, 1)
    arrays(8, 1, 1)
    shapes.append(pltpu.VMEM((22, 22, 8, 128), jnp.int32))
    arrays(16, 16, 1)
    shapes.append(pltpu.VMEM((2, 8, 128), F32))
    shapes.append(pltpu.VMEM((2, 8, 128), F32))
    arrays(16, 4, 1)
    dma = pltpu.SemaphoreType.DMA
    shapes += [dma((12,)), dma((24,)), dma((7, 8)), dma((7, 8)), dma((2, 3)), dma((2, 2)), pltpu.SemaphoreType.REGULAR((3,))]
    return shapes


def per_device(right_side, cotangent, phase):
    shape = jax.ShapeDtypeStruct((2,) + right_side.shape, F32)
    both = pl.pallas_call(
        kernel,
        out_shape=shape,
        in_specs=[pl.BlockSpec(memory_space=pl.ANY)] * 3,
        out_specs=pl.BlockSpec(memory_space=pl.ANY),
        scratch_shapes=scratch_shapes(),
        compiler_params=pltpu.CompilerParams(
            collective_id=0, has_side_effects=True, vmem_limit_bytes=62 * 2**20
        ),
    )(right_side, cotangent, phase)
    return both[0], both[1]


def solution(mesh):
    spec = P("gz", "gy", None)
    return jax.shard_map(
        per_device, mesh=mesh, in_specs=(spec,) * 3, out_specs=(spec,) * 2, check_vma=False
    )
```
